32 devices in a mesh: layer: 4 (over y, x), row: 8 (over z, core).
Axes of the slice: x: 2, y: 2, z: 4, core: 2. Of those that a mesh axis runs over, the one named last changes fastest.
Arguments:
- tokens: bfloat16 [16, 8192], P('row'), may hold values from -6 to 6
- up_weight: bfloat16 [4, 32768, 8192], P('layer', 'row'), may hold values from -6 to 6
- hess_panel: float32 [4, 256, 8192], P('layer', None, 'row'), may hold values from -1 to 2, as said below
- keep_mask: int32 [4, 32768, 256], P('layer', 'row'), may hold values from 0 to 1, as said below
Outputs:
- section_acts: bfloat16 [4, 16, 8192], P('layer', 'row')
- pruned_blocks: bfloat16 [4, 32768, 256], P('layer', 'row')
The draws below stay inside these ranges and needn't reach their ends.
Inputs may be any that keep to these rules, and one draw needn't show every extreme that they name: `keep_mask`: each row has exactly 64 ones in each block of 128 columns. `hess_panel`: zero where the column is below the row; the diagonal lies in [0.5, 2].
All inputs are finite; a program needn't handle non-finite values.
Results may differ from the reference program's by a relative error of at most 0.017.
Values may be sent and summed in bfloat16 or wider, within the bound.
No kernel may reach another device: no remote copies, remote signals or barrier semaphores. Data moves between devices by JAX's collectives and lax.ppermute only.
A program may use at most 384 MiB of HBM per device.

```python
import math
import jax
import jax.numpy as jnp
from jax import lax

D = 8192
FFW = 32768
BLOCK = 128
TOKENS = 16
N_LAYER = 4


def draw_keep_mask(key, part):
    total_rows = N_LAYER * FFW * 2
    row_keys = jax.random.split(key, total_rows)
    orders = jax.vmap(lambda single: jax.random.permutation(single, BLOCK))(row_keys)
    retained = (orders < BLOCK // 2).astype(jnp.int32)
    return retained.reshape(N_LAYER, FFW, 2 * BLOCK)


def draw_hess_panel(key, part):
    key_list = jax.random.split(jax.random.fold_in(key, 17), 4)
    first_key = key_list[0]
    second_key = key_list[1]
    row_key = key_list[2]
    column_key = key_list[3]
    panel_shape = (N_LAYER, 2 * BLOCK, D)
    entries = jnp.clip(jax.random.normal(first_key, panel_shape, jnp.float32), -4.0, 4.0)
    row_index = jnp.arange(2 * BLOCK)[:, None]
    column_index = jnp.arange(D)[None, :]
    factor = jnp.where(column_index < 2 * BLOCK, 0.5 / math.sqrt(BLOCK), 1.0 / math.sqrt(2 * BLOCK))
    row_scale = jax.random.uniform(row_key, (N_LAYER, 2 * BLOCK, 1), jnp.float32, 0.5, 1.5)
    column_scale = jax.random.uniform(column_key, (N_LAYER, 1, D), jnp.float32, 0.5, 1.5)
    coherent = jnp.where(column_index < 2 * BLOCK, 0.08 * row_scale * column_scale, 0.0)
    pivots = jnp.exp(jax.random.uniform(second_key, (N_LAYER, 2 * BLOCK, 1), jnp.float32, math.log(0.5), math.log(2.0)))
    upper = jnp.where(column_index > row_index, entries * factor + coherent, 0.0)
    return (upper + jnp.where(column_index == row_index, pivots, 0.0)).astype(jnp.float32)


def block_levels(stream_key, extent, cuts, smallest, high):
    factor_of = 1.0
    for position, blocks in cuts:
        draws = jax.random.uniform(jax.random.fold_in(jax.random.fold_in(stream_key, 6), position), (blocks,), jnp.float32, smallest / len(cuts), high / len(cuts))
        factor_of = factor_of * jnp.repeat(jnp.exp(draws), extent[position] // blocks).reshape((-1,) + (1,) * (len(extent) - 1 - position))
    return factor_of


def normal_values(rng, extent, spread, bound, cuts=(), held_as=jnp.bfloat16):
    level = block_levels(rng, extent, cuts, -0.22, 0.18) if cuts else 1.0
    values = jax.random.normal(rng, extent, jnp.float32) * spread * level
    return jnp.minimum(jnp.maximum(values, -bound), bound).astype(held_as)


def setup_inputs(seed: int = 0) -> dict:
    streams_of = jax.random.split(jax.random.key(seed), 5)
    tokens = normal_values(streams_of[0], (TOKENS, D), 1.0, 6.0, ((0, 8),))
    up_weight = normal_values(streams_of[1], (N_LAYER, FFW, D), 1.0, 6.0, ((0, 4), (1, 8)))
    hess_panel = draw_hess_panel(jax.random.fold_in(streams_of[4], 71), 0)
    keep_mask = draw_keep_mask(jax.random.fold_in(streams_of[4], 71), 0)
    return dict(tokens=tokens, up_weight=up_weight, hess_panel=hess_panel, keep_mask=keep_mask)


epsilon = 1e-05

def highest_dot(left, right):
    return jnp.dot(left, right, precision=lax.Precision.HIGHEST, preferred_element_type=jnp.float32)

def eliminate(columns_in, pivot_block, retained):
    count = pivot_block.shape[0]
    width_sub = min(16, count)
    inverse = 1.0 / jnp.diagonal(pivot_block)
    dropped = 1.0 - retained.astype(jnp.float32)
    residual = columns_in
    error_list = []
    for start in range(0, count, width_sub):
        finish = start + width_sub
        current = residual[:, start:finish]
        local_errors = []
        for offset in range(width_sub):
            index_col = start + offset
            error = current[:, offset:offset + 1] * dropped[:, index_col:index_col + 1] * inverse[index_col]
            current = current - error * pivot_block[index_col:index_col + 1, start:finish]
            local_errors.append(error)
        sub_errors = jnp.concatenate(local_errors, 1)
        error_list.append(sub_errors)
        pieces = [residual[:, :start], current]
        if finish < count:
            pieces.append(residual[:, finish:] - highest_dot(sub_errors, pivot_block[start:finish, finish:]))
        residual = jnp.concatenate(pieces, 1)
    return (residual, jnp.concatenate(error_list, 1))

def prune_layer(weight, panel, retained):
    width_block = panel.shape[0] // 2
    leading = weight[:, :2 * width_block].astype(jnp.float32)
    first_values, errors_first = eliminate(leading[:, :width_block], panel[:width_block, :width_block], retained[:, :width_block])
    second_in = leading[:, width_block:] - highest_dot(errors_first, panel[:width_block, width_block:2 * width_block])
    second_values, errors_second = eliminate(second_in, panel[width_block:, width_block:2 * width_block], retained[:, width_block:])
    pruned = jnp.concatenate([first_values, second_values], 1).astype(jnp.bfloat16)
    return (pruned, jnp.concatenate([errors_first, errors_second], 1))

def advance(inputs, mixed_weight, remote_panel, errors):
    features = inputs.shape[1]
    leading_count = errors.shape[1]
    product = lax.dot_general(inputs, mixed_weight, (((1,), (1,)), ((), ())), preferred_element_type=jnp.float32)
    panel_inputs = lax.dot_general(inputs[:, leading_count:].astype(jnp.float32), remote_panel, (((1,), (1,)), ((), ())), precision=lax.Precision.HIGHEST, preferred_element_type=jnp.float32)
    correction = lax.dot_general(panel_inputs, errors, (((1,), (1,)), ((), ())), precision=lax.Precision.HIGHEST, preferred_element_type=jnp.float32)
    layer_output = ((product - correction) * features ** (-0.5)).astype(jnp.bfloat16)
    hidden = jax.nn.silu(layer_output.astype(jnp.float32))
    folded = hidden.reshape(inputs.shape[0], -1, features).sum(axis=1)
    combined = inputs.astype(jnp.float32) + folded
    moment = lax.optimization_barrier(jnp.mean(combined * combined, axis=-1, keepdims=True))
    return (combined * lax.rsqrt(moment + epsilon)).astype(jnp.bfloat16)

def reference(tokens, up_weight, hess_panel, keep_mask):
    inputs = tokens
    activations = []
    pruned_list = []
    leading_count = 2 * BLOCK
    for layer_index in range(N_LAYER):
        weight = up_weight[layer_index]
        panel = hess_panel[layer_index]
        pruned, errors = prune_layer(weight, panel[:, :leading_count], keep_mask[layer_index])
        mixed_weight = jnp.concatenate([pruned, weight[:, leading_count:]], 1)
        inputs = advance(inputs, mixed_weight, panel[:, leading_count:], errors)
        activations.append(inputs)
        pruned_list.append(pruned)
    return (jnp.stack(activations), jnp.stack(pruned_list))
```

```python
import functools

import jax
import jax.numpy as jnp
from jax import lax
from jax.experimental import pallas as pl
from jax.experimental.pallas import tpu as pltpu
from jax.sharding import PartitionSpec as P

BLOCK = 128
SUB = 16

epsilon = 1e-05


def passed_along(array, axis, by):
    size = lax.axis_size(axis)
    pairs = [(i, i + by) for i in range(size) if 0 <= i + by < size]
    return lax.ppermute(array, axis, pairs)


def gathered(array, axis):
    size = lax.axis_size(axis)
    copies = jnp.broadcast_to(array[None], (size,) + array.shape)
    return lax.all_to_all(copies, axis, split_axis=0, concat_axis=0)


def nt_dot(left, right):
    return lax.dot_general(
        left, right, (((1,), (1,)), ((), ())), preferred_element_type=jnp.float32
    )


def nn_dot(left, right):
    return jnp.dot(left, right, preferred_element_type=jnp.float32)


def split_halves(value):
    high = value.astype(jnp.bfloat16)
    low = (value - high.astype(jnp.float32)).astype(jnp.bfloat16)
    return high, low


def identity(count):
    row = lax.broadcasted_iota(jnp.int32, (count, count), 0)
    column = lax.broadcasted_iota(jnp.int32, (count, count), 1)
    return jnp.where(row == column, 1.0, 0.0).astype(jnp.bfloat16)


def eliminate_kernel(scalar_ref, inverse_ref, inner_ref, cross_ref, weight_ref, mask_ref,
                     pruned_ref, aux_ref, state, dropped, errors):
    count = 2 * BLOCK
    depth = count * 8
    sheets = state.shape[0] // depth
    lanes = sheets * 128
    spots = [(g, q, slice((g * sheets + q) * 128, (g * sheets + q + 1) * 128))
             for g in range(8) for q in range(sheets)]

    def place(g, q, first, size):
        return pl.ds(q * depth + first * 8 + g, size, stride=8)

    def plane(q, j):
        return slice(q * depth + j * 8, q * depth + (j + 1) * 8)

    eye = identity(count)
    columns = nt_dot(eye, weight_ref[...])
    drops = nt_dot(eye, (1 - mask_ref[...]).astype(jnp.float32).astype(jnp.bfloat16))
    for g, q, where in spots:
        state[place(g, q, 0, count), :] = columns[:, where]
        dropped[place(g, q, 0, count), :] = drops[:, where]

    def stacked(first, size):
        wide = jnp.concatenate([errors[place(g, q, first, size), :] for g, q, _ in spots], 1)
        return jnp.concatenate(split_halves(wide), 0)

    def subtract(product, first, size):
        for g, q, where in spots:
            at = place(g, q, first, size)
            state[at, :] = state[at, :] - product[:, where]

    for block in range(2):
        for part in range(BLOCK // SUB):
            first = block * BLOCK + part * SUB
            planes = [[state[plane(q, first + i), :] for q in range(sheets)] for i in range(SUB)]
            for i in range(SUB):
                j = first + i
                inverse = inverse_ref[j]
                error = []
                for q in range(sheets):
                    lost = planes[i][q] * dropped[plane(q, j), :]
                    error.append(lost * inverse)
                    state[plane(q, j), :] = planes[i][q] - lost
                    errors[plane(q, j), :] = error[q]
                for k in range(i + 1, SUB):
                    scalar = scalar_ref[j * SUB + k]
                    for q in range(sheets):
                        planes[k][q] = planes[k][q] - error[q] * scalar
            after = first + SUB
            left = (block + 1) * BLOCK - after
            if left:
                factor = inner_ref[block * (BLOCK // SUB) + part, after : after + left, :]
                subtract(nn_dot(factor, stacked(first, SUB)), after, left)
        if block == 0:
            subtract(nn_dot(cross_ref[...], stacked(0, BLOCK)), BLOCK, BLOCK)

    small = identity(128)
    for g, q, where in spots:
        kept = state[place(g, q, 0, count), :].astype(jnp.bfloat16)
        high, low = split_halves(errors[place(g, q, 0, count), :])
        aux_ref[0:count, where] = kept
        aux_ref[count : 2 * count, where] = high
        aux_ref[2 * count : 3 * count, where] = low
        pruned_ref[where, :] = nt_dot(small, kept).astype(jnp.bfloat16)


def eliminate(weight, factor, mask):
    count = 2 * BLOCK
    given = weight.shape[0]
    rows = pl.cdiv(given, 1024) * 1024
    if rows != given:
        more = ((0, rows - given), (0, 0))
        weight, mask = jnp.pad(weight[:, :count], more), jnp.pad(mask, more)
    tile = 1024 if rows % 2048 else 2048
    subs = count // SUB
    wide = factor.astype(jnp.float32)
    row = lax.broadcasted_iota(jnp.int32, wide.shape, 0)
    column = lax.broadcasted_iota(jnp.int32, wide.shape, 1)
    inverse = 1.0 / jnp.sum(jnp.where(row == column, wide, 0.0), axis=1)
    near = jnp.where(row // SUB == column // SUB, wide, 0.0)
    scalars = near.reshape(count, subs, SUB).sum(axis=1).reshape(-1)
    columns = factor.T.reshape(count, subs, SUB).transpose(1, 0, 2)
    inner = jnp.concatenate([columns, columns], 2)
    cross = factor[:BLOCK, BLOCK:].T
    cross = jnp.concatenate([cross, cross], 1)
    smem = pl.BlockSpec(memory_space=pltpu.SMEM)
    pruned, aux = pl.pallas_call(
        eliminate_kernel,
        grid=(rows // tile,),
        in_specs=[
            smem,
            smem,
            pl.BlockSpec((subs, count, 2 * SUB), lambda i: (0, 0, 0)),
            pl.BlockSpec((BLOCK, count), lambda i: (0, 0)),
            pl.BlockSpec((tile, count), lambda i: (i, 0)),
            pl.BlockSpec((tile, count), lambda i: (i, 0)),
        ],
        out_specs=[
            pl.BlockSpec((tile, count), lambda i: (i, 0)),
            pl.BlockSpec((3 * count, tile), lambda i: (0, i)),
        ],
        out_shape=[
            jax.ShapeDtypeStruct((rows, count), jnp.bfloat16),
            jax.ShapeDtypeStruct((3 * count, rows), jnp.bfloat16),
        ],
        scratch_shapes=[pltpu.VMEM((tile * count // 128, 128), jnp.float32)] * 3,
        compiler_params=pltpu.CompilerParams(vmem_limit_bytes=52 * 1024 * 1024),
        cost_estimate=pl.CostEstimate(
            flops=2 * rows * count * count, bytes_accessed=rows * count * 14, transcendentals=0
        ),
        name="eliminate",
    )(scalars, inverse, inner, cross, weight, mask)
    return pruned[:given], aux[:, :given]


def combine_kernel(scale, product_ref, lead_ref, panel_ref, aux_ref, out_ref):
    count = 2 * BLOCK
    tokens = product_ref.shape[0]
    high, low = split_halves(panel_ref[...])
    both = nn_dot(jnp.concatenate([high, low], 0), aux_ref[count : 2 * count, :])
    correction = both[:tokens] + both[tokens:] + nn_dot(high, aux_ref[2 * count :, :])
    pruned = nn_dot(lead_ref[...], aux_ref[0:count, :])
    out_ref[...] = ((product_ref[...] + pruned - correction) * scale).astype(jnp.bfloat16)


def combine(product, lead, panel_inputs, aux, scale):
    tokens, rows = product.shape
    count = 2 * BLOCK
    tile = min(1024, rows)
    return pl.pallas_call(
        functools.partial(combine_kernel, scale),
        grid=(rows // tile,),
        in_specs=[
            pl.BlockSpec((tokens, tile), lambda i: (0, i)),
            pl.BlockSpec((tokens, count), lambda i: (0, 0)),
            pl.BlockSpec((tokens, count), lambda i: (0, 0)),
            pl.BlockSpec((3 * count, tile), lambda i: (0, i)),
        ],
        out_specs=pl.BlockSpec((tokens, tile), lambda i: (0, i)),
        out_shape=jax.ShapeDtypeStruct((tokens, rows), jnp.bfloat16),
        compiler_params=pltpu.CompilerParams(vmem_limit_bytes=24 * 1024 * 1024),
        cost_estimate=pl.CostEstimate(
            flops=8 * tokens * rows * count, bytes_accessed=rows * count * 6, transcendentals=0
        ),
        name="combine",
    )(product, lead, panel_inputs, aux)


def per_device(tokens, up_weight, hess_panel, keep_mask):
    weight = up_weight[0]
    local_panel = hess_panel[0].astype(jnp.bfloat16)
    count = 2 * BLOCK
    features = weight.shape[1]
    row_size = lax.axis_size("row")
    own = tokens.shape[0]
    position = lax.axis_index("layer")
    depth = lax.axis_size("layer")

    width = min(count, local_panel.shape[1])
    share = count // row_size
    factor_share = local_panel[:, :width].reshape(row_size, share * width // count, count)
    token_share = jnp.broadcast_to(
        tokens.reshape(1, own * features // count, count), (row_size, own * features // count, count)
    )
    first = lax.all_to_all(
        jnp.concatenate([token_share, factor_share], 1), "row", split_axis=0, concat_axis=0
    )
    cut = own * features // count
    portion = first[:, :cut].reshape(row_size * own, features)
    owned = [first[o, cut:].reshape(share, width) for o in range(count // width)]
    factor = gathered(jnp.concatenate(owned, 1), "row").reshape(count, count)
    full_panel = lax.all_gather(local_panel, "row", axis=1, tiled=True)

    pruned, aux = eliminate(weight, factor, keep_mask[0])

    section_input = tokens
    results = jnp.zeros_like(tokens)
    for turn in range(depth):
        if turn:
            portion = gathered(section_input, "row").reshape(row_size * own, features)
        lead = portion[:, :count]
        column = lax.broadcasted_iota(jnp.int32, portion.shape, 1)
        rest = jnp.where(column < count, jnp.zeros_like(portion), portion)
        product = nt_dot(rest, weight)
        panel_inputs = nt_dot(rest, full_panel)
        layer_output = combine(product, lead, panel_inputs, aux, features ** (-0.5))
        spread = lax.all_to_all(layer_output, "row", split_axis=0, concat_axis=1, tiled=True)
        hidden = jax.nn.silu(spread.astype(jnp.float32))
        folded = hidden.reshape(own, -1, features).sum(axis=1)
        combined = section_input.astype(jnp.float32) + folded
        moment = jnp.mean(combined * combined, axis=-1, keepdims=True)
        produced = (combined * lax.rsqrt(moment + epsilon)).astype(jnp.bfloat16)
        results = jnp.where(position == turn, produced, results)
        if turn + 1 < depth:
            section_input = passed_along(produced, "layer", 1)
    return (results[None], pruned[None])


def solution(mesh):
    in_specs = (
        P("row", None),
        P("layer", "row", None),
        P("layer", None, "row"),
        P("layer", "row", None),
    )
    out_specs = (P("layer", "row", None), P("layer", "row", None))
    return jax.shard_map(
        per_device, mesh=mesh, in_specs=in_specs, out_specs=out_specs, check_vma=False
    )
```

```python
import functools

import jax
import jax.numpy as jnp
from jax import lax
from jax.experimental import pallas as pl
from jax.experimental.pallas import tpu as pltpu
from jax.sharding import PartitionSpec as P

BLOCK = 128
SUB = 16

epsilon = 1e-05


def passed_along(array, axis, by):
    size = lax.axis_size(axis)
    pairs = [(i, i + by) for i in range(size) if 0 <= i + by < size]
    return lax.ppermute(array, axis, pairs)


def gathered(array, axis):
    size = lax.axis_size(axis)
    copies = jnp.broadcast_to(array[None], (size,) + array.shape)
    return lax.all_to_all(copies, axis, split_axis=0, concat_axis=0)


def nt_dot(left, right):
    return lax.dot_general(
        left, right, (((1,), (1,)), ((), ())), preferred_element_type=jnp.float32
    )


def nn_dot(left, right):
    return jnp.dot(left, right, preferred_element_type=jnp.float32)


def split_halves(value):
    high = value.astype(jnp.bfloat16)
    low = (value - high.astype(jnp.float32)).astype(jnp.bfloat16)
    return high, low


def identity(count):
    row = lax.broadcasted_iota(jnp.int32, (count, count), 0)
    column = lax.broadcasted_iota(jnp.int32, (count, count), 1)
    return jnp.where(row == column, 1.0, 0.0).astype(jnp.bfloat16)


def eliminate_kernel(scalar_ref, inverse_ref, inner_ref, cross_ref, weight_ref, mask_ref,
                     pruned_ref, aux_ref, state, dropped, errors):
    count = 2 * BLOCK
    depth = count * 8
    sheets = state.shape[0] // depth
    lanes = sheets * 128
    spots = [(g, q, slice((g * sheets + q) * 128, (g * sheets + q + 1) * 128))
             for g in range(8) for q in range(sheets)]

    def place(g, q, first, size):
        return pl.ds(q * depth + first * 8 + g, size, stride=8)

    def plane(q, j):
        return slice(q * depth + j * 8, q * depth + (j + 1) * 8)

    eye = identity(count)
    columns = nt_dot(eye, weight_ref[...])
    drops = nt_dot(eye, (1 - mask_ref[...]).astype(jnp.float32).astype(jnp.bfloat16))
    for g, q, where in spots:
        state[place(g, q, 0, count), :] = columns[:, where]
        dropped[place(g, q, 0, count), :] = drops[:, where]

    def stacked(first, size):
        wide = jnp.concatenate([errors[place(g, q, first, size), :] for g, q, _ in spots], 1)
        return jnp.concatenate(split_halves(wide), 0)

    def subtract(product, first, size):
        for g, q, where in spots:
            at = place(g, q, first, size)
            state[at, :] = state[at, :] - product[:, where]

    for block in range(2):
        for part in range(BLOCK // SUB):
            first = block * BLOCK + part * SUB
            planes = [[state[plane(q, first + i), :] for q in range(sheets)] for i in range(SUB)]
            for i in range(SUB):
                j = first + i
                inverse = inverse_ref[j]
                error = []
                for q in range(sheets):
                    lost = planes[i][q] * dropped[plane(q, j), :]
                    error.append(lost * inverse)
                    state[plane(q, j), :] = planes[i][q] - lost
                    errors[plane(q, j), :] = error[q]
                for k in range(i + 1, SUB):
                    scalar = scalar_ref[j * SUB + k]
                    for q in range(sheets):
                        planes[k][q] = planes[k][q] - error[q] * scalar
            after = first + SUB
            left = (block + 1) * BLOCK - after
            if left:
                factor = inner_ref[block * (BLOCK // SUB) + part, after : after + left, :]
                subtract(nn_dot(factor, stacked(first, SUB)), after, left)
        if block == 0:
            subtract(nn_dot(cross_ref[...], stacked(0, BLOCK)), BLOCK, BLOCK)

    small = identity(128)
    for g, q, where in spots:
        kept = state[place(g, q, 0, count), :].astype(jnp.bfloat16)
        aux_ref[0:count, where] = kept
        aux_ref[count:, where] = errors[place(g, q, 0, count), :].astype(jnp.bfloat16)
        pruned_ref[where, :] = nt_dot(small, kept).astype(jnp.bfloat16)


def eliminate(weight, factor, mask):
    count = 2 * BLOCK
    given = weight.shape[0]
    rows = pl.cdiv(given, 1024) * 1024
    if rows != given:
        more = ((0, rows - given), (0, 0))
        weight, mask = jnp.pad(weight[:, :count], more), jnp.pad(mask, more)
    tile = 1024 if rows % 2048 else 2048
    subs = count // SUB
    wide = factor.astype(jnp.float32)
    row = lax.broadcasted_iota(jnp.int32, wide.shape, 0)
    column = lax.broadcasted_iota(jnp.int32, wide.shape, 1)
    inverse = 1.0 / jnp.sum(jnp.where(row == column, wide, 0.0), axis=1)
    near = jnp.where(row // SUB == column // SUB, wide, 0.0)
    scalars = near.reshape(count, subs, SUB).sum(axis=1).reshape(-1)
    columns = factor.T.reshape(count, subs, SUB).transpose(1, 0, 2)
    inner = jnp.concatenate([columns, columns], 2)
    cross = factor[:BLOCK, BLOCK:].T
    cross = jnp.concatenate([cross, cross], 1)
    smem = pl.BlockSpec(memory_space=pltpu.SMEM)
    pruned, aux = pl.pallas_call(
        eliminate_kernel,
        grid=(rows // tile,),
        in_specs=[
            smem,
            smem,
            pl.BlockSpec((subs, count, 2 * SUB), lambda i: (0, 0, 0)),
            pl.BlockSpec((BLOCK, count), lambda i: (0, 0)),
            pl.BlockSpec((tile, count), lambda i: (i, 0)),
            pl.BlockSpec((tile, count), lambda i: (i, 0)),
        ],
        out_specs=[
            pl.BlockSpec((tile, count), lambda i: (i, 0)),
            pl.BlockSpec((2 * count, tile), lambda i: (0, i)),
        ],
        out_shape=[
            jax.ShapeDtypeStruct((rows, count), jnp.bfloat16),
            jax.ShapeDtypeStruct((2 * count, rows), jnp.bfloat16),
        ],
        scratch_shapes=[pltpu.VMEM((tile * count // 128, 128), jnp.float32)] * 3,
        compiler_params=pltpu.CompilerParams(vmem_limit_bytes=26 * 1024 * 1024),
        cost_estimate=pl.CostEstimate(
            flops=2 * rows * count * count, bytes_accessed=rows * count * 12, transcendentals=0
        ),
        name="eliminate",
    )(scalars, inverse, inner, cross, weight, mask)
    return pruned[:given], aux[:, :given]


def corrected(lead, panel_inputs, aux_ref, place):
    count = 2 * BLOCK
    tokens = lead.shape[0]
    both = nn_dot(jnp.concatenate(split_halves(panel_inputs), 0), aux_ref[count:, place])
    return nn_dot(lead, aux_ref[0:count, place]) - both[:tokens] - both[tokens:]


def combine_kernel(scale, product_ref, lead_ref, panel_ref, aux_ref, out_ref):
    change = corrected(lead_ref[...], panel_ref[...], aux_ref, slice(None))
    out_ref[...] = ((product_ref[...] + change) * scale).astype(jnp.bfloat16)


def combine(product, lead, panel_inputs, aux, scale):
    tokens, rows = product.shape
    count = 2 * BLOCK
    tile = min(1024, rows)
    return pl.pallas_call(
        functools.partial(combine_kernel, scale),
        grid=(rows // tile,),
        in_specs=[
            pl.BlockSpec((tokens, tile), lambda i: (0, i)),
            pl.BlockSpec((tokens, count), lambda i: (0, 0)),
            pl.BlockSpec((tokens, count), lambda i: (0, 0)),
            pl.BlockSpec((2 * count, tile), lambda i: (0, i)),
        ],
        out_specs=pl.BlockSpec((tokens, tile), lambda i: (0, i)),
        out_shape=jax.ShapeDtypeStruct((tokens, rows), jnp.bfloat16),
        compiler_params=pltpu.CompilerParams(vmem_limit_bytes=8 * 1024 * 1024),
        cost_estimate=pl.CostEstimate(
            flops=8 * tokens * rows * count, bytes_accessed=rows * count * 4, transcendentals=0
        ),
        name="combine",
    )(product, lead, panel_inputs, aux)


def streaming(weight_ref, ring, ring_sems):
    slots, chunk, width = ring.shape
    skipped = weight_ref.shape[1] - width
    total = weight_ref.shape[0] // chunk

    def copy(index, slot):
        rows = pl.ds(pl.multiple_of(index * chunk, chunk), chunk)
        return pltpu.make_async_copy(
            weight_ref.at[rows, pl.ds(skipped, width)], ring.at[slot], ring_sems.at[slot]
        )

    def run(inputs, use):
        def step(index, _):
            slot = lax.rem(index, slots)
            copy(index, slot).wait()
            use(pl.ds(pl.multiple_of(index * chunk, chunk), chunk), nt_dot(inputs, ring[slot]))

            @pl.when(index + slots < total)
            def _():
                copy(index + slots, slot).start()

            return 0

        lax.fori_loop(0, total, step, 0)

    def begin():
        for index in range(slots):
            copy(index, index).start()

    return begin, run


def first_kernel(inputs_ref, weight_ref, product_ref, ring, ring_sems):
    skipped = weight_ref.shape[1] - ring.shape[2]
    begin, run = streaming(weight_ref, ring, ring_sems)
    begin()

    def use(rows, product):
        product_ref[:, rows] = product

    run(inputs_ref[:, skipped:], use)


def ring_shape(rows, width):
    chunk = min(256, rows // 2)
    return min(6, rows // chunk), chunk, width


def first_product(inputs, weight):
    tokens, features = inputs.shape
    rows = weight.shape[0]
    width = features - 2 * BLOCK
    ring = ring_shape(rows, width)
    return pl.pallas_call(
        first_kernel,
        in_specs=[
            pl.BlockSpec(memory_space=pltpu.VMEM),
            pl.BlockSpec(memory_space=pl.ANY),
        ],
        out_specs=pl.BlockSpec(memory_space=pltpu.VMEM),
        out_shape=jax.ShapeDtypeStruct((tokens, rows), jnp.float32),
        scratch_shapes=[pltpu.VMEM(ring, jnp.bfloat16), pltpu.SemaphoreType.DMA((ring[0],))],
        compiler_params=pltpu.CompilerParams(vmem_limit_bytes=32 * 1024 * 1024),
        cost_estimate=pl.CostEstimate(
            flops=2 * tokens * rows * width, bytes_accessed=rows * width * 2, transcendentals=0
        ),
        name="first_product",
    )(inputs, weight)


def turn_kernel(scale, inputs_ref, weight_ref, panel_ref, aux_ref, out_ref, ring, panel, aux,
                change, ring_sems, side_sems):
    width = ring.shape[2]
    skipped = weight_ref.shape[1] - width
    begin, run = streaming(weight_ref, ring, ring_sems)
    panel_copy = pltpu.make_async_copy(
        panel_ref.at[:, pl.ds(skipped, width)], panel, side_sems.at[0]
    )
    aux_copy = pltpu.make_async_copy(aux_ref, aux, side_sems.at[1])
    panel_copy.start()
    aux_copy.start()
    begin()
    panel_copy.wait()
    panel_inputs = nt_dot(inputs_ref[:, skipped:], panel[...])
    aux_copy.wait()
    rows = change.shape[1]
    tile = min(1024, rows)
    for at in range(0, rows, tile):
        place = slice(at, at + tile)
        change[:, place] = corrected(inputs_ref[:, :skipped], panel_inputs, aux, place)

    def use(place, product):
        out_ref[:, place] = ((product + change[:, place]) * scale).astype(jnp.bfloat16)

    run(inputs_ref[:, skipped:], use)


def turn_product(inputs, weight, panel, aux, scale):
    tokens, features = inputs.shape
    rows = weight.shape[0]
    count = 2 * BLOCK
    width = features - count
    ring = ring_shape(rows, width)
    return pl.pallas_call(
        functools.partial(turn_kernel, scale),
        in_specs=[pl.BlockSpec(memory_space=pltpu.VMEM)] + [pl.BlockSpec(memory_space=pl.ANY)] * 3,
        out_specs=pl.BlockSpec(memory_space=pltpu.VMEM),
        out_shape=jax.ShapeDtypeStruct((tokens, rows), jnp.bfloat16),
        scratch_shapes=[
            pltpu.VMEM(ring, jnp.bfloat16),
            pltpu.VMEM((count, width), jnp.bfloat16),
            pltpu.VMEM(aux.shape, jnp.bfloat16),
            pltpu.VMEM((tokens, rows), jnp.float32),
            pltpu.SemaphoreType.DMA((ring[0],)),
            pltpu.SemaphoreType.DMA((2,)),
        ],
        compiler_params=pltpu.CompilerParams(vmem_limit_bytes=44 * 1024 * 1024),
        cost_estimate=pl.CostEstimate(
            flops=2 * tokens * rows * features, bytes_accessed=rows * width * 2, transcendentals=0
        ),
        name="turn_product",
    )(inputs, weight, panel, aux)


def per_device(tokens, up_weight, hess_panel, keep_mask):
    weight = up_weight[0]
    local_panel = hess_panel[0].astype(jnp.bfloat16)
    count = 2 * BLOCK
    features = weight.shape[1]
    scale = features ** (-0.5)
    row_size = lax.axis_size("row")
    own = tokens.shape[0]
    held = local_panel.shape[1]
    position = lax.axis_index("layer")
    depth = lax.axis_size("layer")
    start = lax.axis_index("row") * held

    width = min(count, held)
    share = count // row_size
    factor_share = local_panel[:, :width].reshape(row_size, share * width // count, count)
    cut = own * features // count
    token_share = jnp.broadcast_to(tokens.reshape(1, cut, count), (row_size, cut, count))
    first = lax.all_to_all(
        jnp.concatenate([token_share, factor_share], 1), "row", split_axis=0, concat_axis=0
    )
    first, local_panel = lax.optimization_barrier((first, local_panel))
    portion = first[:, :cut].reshape(row_size * own, features)
    full_panel = lax.all_gather(local_panel, "row", axis=1, tiled=True)

    owned = [first[o, cut:].reshape(share, width) for o in range(count // width)]
    column = lax.broadcasted_iota(jnp.int32, local_panel.shape, 1) + start
    remote = jnp.where(column < count, jnp.zeros_like(local_panel), local_panel)
    partial_sum = nt_dot(lax.dynamic_slice_in_dim(portion, start, held, 1), remote)
    shares = jnp.concatenate([jnp.concatenate(owned, 1), *split_halves(partial_sum)], 0)
    shares, portion = lax.optimization_barrier((shares, portion))
    second = gathered(shares, "row")
    factor = second[:, :share].reshape(count, count)
    sums = second[:, share:].astype(jnp.float32).reshape(row_size, 2, row_size * own, count)

    product = first_product(portion, weight)
    pruned, aux = eliminate(weight, factor, keep_mask[0])

    section_input = tokens
    results = jnp.zeros_like(tokens)
    for turn in range(depth):
        if turn:
            portion = gathered(section_input, "row").reshape(row_size * own, features)
            layer_output = turn_product(portion, weight, full_panel, aux, scale)
        else:
            layer_output = combine(product, portion[:, :count], sums.sum(axis=(0, 1)), aux, scale)
        spread = lax.all_to_all(layer_output, "row", split_axis=0, concat_axis=1, tiled=True)
        hidden = jax.nn.silu(spread.astype(jnp.float32))
        folded = hidden.reshape(own, -1, features).sum(axis=1)
        combined = section_input.astype(jnp.float32) + folded
        moment = jnp.mean(combined * combined, axis=-1, keepdims=True)
        produced = (combined * lax.rsqrt(moment + epsilon)).astype(jnp.bfloat16)
        results = jnp.where(position == turn, produced, results)
        if turn + 1 < depth:
            section_input = passed_along(produced, "layer", 1)
    return (results[None], pruned[None])


def solution(mesh):
    in_specs = (
        P("row", None),
        P("layer", "row", None),
        P("layer", None, "row"),
        P("layer", "row", None),
    )
    out_specs = (P("layer", "row", None), P("layer", "row", None))
    return jax.shard_map(
        per_device, mesh=mesh, in_specs=in_specs, out_specs=out_specs, check_vma=False
    )
```

```python
import functools

import jax
import jax.numpy as jnp
from jax import lax
from jax.experimental import pallas as pl
from jax.experimental.pallas import tpu as pltpu
from jax.sharding import PartitionSpec as P

BLOCK = 128
SUB = 16
HELD = 7
ELIMINATE_VMEM = 56 * 1024 * 1024
TURN_VMEM = 32 * 1024 * 1024

epsilon = 1e-05


def gathered(array, axis):
    size = lax.axis_size(axis)
    copies = jnp.broadcast_to(array[None], (size,) + array.shape)
    return lax.all_to_all(copies, axis, split_axis=0, concat_axis=0)


def nt_dot(left, right):
    return lax.dot_general(
        left, right, (((1,), (1,)), ((), ())), preferred_element_type=jnp.float32
    )


def nn_dot(left, right):
    return jnp.dot(left, right, preferred_element_type=jnp.float32)


def split_halves(value):
    high = value.astype(jnp.bfloat16)
    low = (value - high.astype(jnp.float32)).astype(jnp.bfloat16)
    return high, low


def identity(count):
    row = lax.broadcasted_iota(jnp.int32, (count, count), 0)
    column = lax.broadcasted_iota(jnp.int32, (count, count), 1)
    return jnp.where(row == column, 1.0, 0.0).astype(jnp.bfloat16)


def eliminate_kernel(scalar_ref, inverse_ref, inner_ref, cross_ref, weight_ref, mask_ref,
                     pruned_ref, aux_ref, state, dropped, errors):
    count = 2 * BLOCK
    depth = count * 8
    sheets = state.shape[0] // depth
    lanes = sheets * 128
    spots = [(g, q, slice((g * sheets + q) * 128, (g * sheets + q + 1) * 128))
             for g in range(8) for q in range(sheets)]

    def place(g, q, first, size):
        return pl.ds(q * depth + first * 8 + g, size, stride=8)

    def plane(q, j):
        return slice(q * depth + j * 8, q * depth + (j + 1) * 8)

    eye = identity(count)
    columns = nt_dot(eye, weight_ref[...])
    drops = nt_dot(eye, (1 - mask_ref[...]).astype(jnp.float32).astype(jnp.bfloat16))
    for g, q, where in spots:
        state[place(g, q, 0, count), :] = columns[:, where]
        dropped[place(g, q, 0, count), :] = drops[:, where]

    def stacked(first, size):
        wide = jnp.concatenate([errors[place(g, q, first, size), :] for g, q, _ in spots], 1)
        return jnp.concatenate(split_halves(wide), 0)

    def subtract(product, first, size):
        for g, q, where in spots:
            at = place(g, q, first, size)
            state[at, :] = state[at, :] - product[:, where]

    for block in range(2):
        for part in range(BLOCK // SUB):
            first = block * BLOCK + part * SUB
            planes = [[state[plane(q, first + i), :] for q in range(sheets)] for i in range(SUB)]
            for i in range(SUB):
                j = first + i
                inverse = inverse_ref[j]
                error = []
                for q in range(sheets):
                    lost = planes[i][q] * dropped[plane(q, j), :]
                    error.append(lost * inverse)
                    state[plane(q, j), :] = planes[i][q] - lost
                    errors[plane(q, j), :] = error[q]
                for k in range(i + 1, SUB):
                    scalar = scalar_ref[j * SUB + k]
                    for q in range(sheets):
                        planes[k][q] = planes[k][q] - error[q] * scalar
            after = first + SUB
            left = (block + 1) * BLOCK - after
            if left:
                factor = inner_ref[block * (BLOCK // SUB) + part, after : after + left, :]
                subtract(nn_dot(factor, stacked(first, SUB)), after, left)
        if block == 0:
            subtract(nn_dot(cross_ref[...], stacked(0, BLOCK)), BLOCK, BLOCK)

    small = identity(128)
    for g, q, where in spots:
        kept = state[place(g, q, 0, count), :].astype(jnp.bfloat16)
        aux_ref[0:count, where] = kept
        aux_ref[count:, where] = errors[place(g, q, 0, count), :].astype(jnp.bfloat16)
        pruned_ref[where, :] = nt_dot(small, kept).astype(jnp.bfloat16)


def eliminate(weight, factor, mask):
    count = 2 * BLOCK
    given = weight.shape[0]
    rows = pl.cdiv(given, 1024) * 1024
    if rows != given:
        more = ((0, rows - given), (0, 0))
        weight, mask = jnp.pad(weight[:, :count], more), jnp.pad(mask, more)
    tile = 1024 if rows % 2048 else 2048
    subs = count // SUB
    wide = factor.astype(jnp.float32)
    row = lax.broadcasted_iota(jnp.int32, wide.shape, 0)
    column = lax.broadcasted_iota(jnp.int32, wide.shape, 1)
    inverse = 1.0 / jnp.sum(jnp.where(row == column, wide, 0.0), axis=1)
    near = jnp.where(row // SUB == column // SUB, wide, 0.0)
    scalars = near.reshape(count, subs, SUB).sum(axis=1).reshape(-1)
    columns = factor.T.reshape(count, subs, SUB).transpose(1, 0, 2)
    inner = jnp.concatenate([columns, columns], 2)
    cross = factor[:BLOCK, BLOCK:].T
    cross = jnp.concatenate([cross, cross], 1)
    smem = pl.BlockSpec(memory_space=pltpu.SMEM)
    pruned, aux = pl.pallas_call(
        eliminate_kernel,
        grid=(rows // tile,),
        in_specs=[
            smem,
            smem,
            pl.BlockSpec((subs, count, 2 * SUB), lambda i: (0, 0, 0)),
            pl.BlockSpec((BLOCK, count), lambda i: (0, 0)),
            pl.BlockSpec((tile, count), lambda i: (i, 0)),
            pl.BlockSpec((tile, count), lambda i: (i, 0)),
        ],
        out_specs=[
            pl.BlockSpec((tile, count), lambda i: (i, 0)),
            pl.BlockSpec((2 * count, tile), lambda i: (0, i)),
        ],
        out_shape=[
            jax.ShapeDtypeStruct((rows, count), jnp.bfloat16),
            jax.ShapeDtypeStruct((2 * count, rows), jnp.bfloat16),
        ],
        scratch_shapes=[pltpu.VMEM((tile * count // 128, 128), jnp.float32)] * 3,
        compiler_params=pltpu.CompilerParams(vmem_limit_bytes=ELIMINATE_VMEM),
        cost_estimate=pl.CostEstimate(
            flops=2 * rows * count * count, bytes_accessed=rows * count * 12, transcendentals=0
        ),
        name="eliminate",
    )(scalars, inverse, inner, cross, weight, mask)
    return pruned[:given], aux[:, :given]


def corrected(lead, panel_inputs, aux_ref, place):
    count = 2 * BLOCK
    tokens = lead.shape[0]
    both = nn_dot(jnp.concatenate(split_halves(panel_inputs), 0), aux_ref[count:, place])
    return nn_dot(lead, aux_ref[0:count, place]) - both[:tokens] - both[tokens:]


def hand_out(out_ref, value, inputs, where_ref, place, scale):
    units = (value * scale).astype(jnp.bfloat16).astype(jnp.float32)
    units = units / (1.0 + jnp.exp(-units))
    first, size = place
    at = pl.ds(pl.multiple_of(where_ref[0] + first, 128), size)
    units = units + inputs[:, at].astype(jnp.float32) * where_ref[1].astype(jnp.float32)
    copies, own, _ = out_ref.shape
    peers = value.shape[0] // own
    for peer in range(peers):
        piece = units[peer * own : (peer + 1) * own].astype(jnp.bfloat16)
        for copy in range(peer, copies, peers):
            out_ref[copy, :, pl.ds(first, size)] = piece


def combine_kernel(scale, where_ref, product_ref, inputs_ref, panel_ref, aux_ref, out_ref):
    count = 2 * BLOCK
    rows = product_ref.shape[1]
    tile = min(1024, rows)
    for first in range(0, rows, tile):
        place = slice(first, first + tile)
        change = corrected(inputs_ref[:, :count], panel_ref[...], aux_ref, place)
        value = product_ref[:, place] + change
        hand_out(out_ref, value, inputs_ref, where_ref, (first, tile), scale)


def combine(where, product, inputs, panel_inputs, aux, scale, out_shape):
    tokens, rows = product.shape
    count = 2 * BLOCK
    return pl.pallas_call(
        functools.partial(combine_kernel, scale),
        in_specs=[pl.BlockSpec(memory_space=pltpu.SMEM)] + [pl.BlockSpec(memory_space=pltpu.VMEM)] * 4,
        out_specs=pl.BlockSpec(memory_space=pltpu.VMEM),
        out_shape=out_shape,
        compiler_params=pltpu.CompilerParams(vmem_limit_bytes=16 * 1024 * 1024),
        cost_estimate=pl.CostEstimate(
            flops=8 * tokens * rows * count, bytes_accessed=rows * count * 4, transcendentals=0
        ),
        name="combine",
    )(where, product, inputs, panel_inputs, aux)


def fold_kernel(spread_ref, copies_ref, produced_ref):
    peers, own, features = copies_ref.shape
    rows = spread_ref.shape[2]
    parts = []
    for first in range(0, features, rows):
        part = None
        for peer in range(peers):
            if peer * rows % features == first:
                units = spread_ref[peer].astype(jnp.float32)
                part = units if part is None else part + units
        parts.append(part)
    combined = jnp.concatenate(parts, 1)
    moment = jnp.sum(combined * combined, axis=1, keepdims=True) * (1.0 / features)
    produced = (combined * lax.rsqrt(moment + epsilon)).astype(jnp.bfloat16)
    produced_ref[...] = produced
    for peer in range(peers):
        copies_ref[peer] = produced


def fold(spread, peers, features):
    own = spread.shape[1]
    return pl.pallas_call(
        fold_kernel,
        in_specs=[pl.BlockSpec(memory_space=pltpu.VMEM)],
        out_specs=[pl.BlockSpec(memory_space=pltpu.VMEM)] * 2,
        out_shape=[
            jax.ShapeDtypeStruct((peers, own, features), jnp.bfloat16),
            jax.ShapeDtypeStruct((own, features), jnp.bfloat16),
        ],
        compiler_params=pltpu.CompilerParams(vmem_limit_bytes=8 * 1024 * 1024),
        name="fold",
    )(spread)


def streaming(weight_ref, ring, ring_sems):
    slots, chunk, width = ring.shape
    skipped = weight_ref.shape[1] - width
    total = weight_ref.shape[0] // chunk

    def copy(index, slot):
        rows = pl.ds(pl.multiple_of(index * chunk, chunk), chunk)
        return pltpu.make_async_copy(
            weight_ref.at[rows, pl.ds(skipped, width)], ring.at[slot], ring_sems.at[slot]
        )

    def run(inputs, use):
        def step(index, _):
            slot = lax.rem(index, slots)
            copy(index, slot).wait()
            use(pl.ds(pl.multiple_of(index * chunk, chunk), chunk), nt_dot(inputs, ring[slot]))

            @pl.when(index + slots < total)
            def _():
                copy(index + slots, slot).start()

            return 0

        lax.fori_loop(0, total, step, 0)

    def begin():
        for index in range(slots):
            copy(index, index).start()

    return begin, run


def first_kernel(inputs_ref, weight_ref, product_ref, ring, ring_sems):
    skipped = weight_ref.shape[1] - ring.shape[2]
    begin, run = streaming(weight_ref, ring, ring_sems)
    begin()

    def use(rows, product):
        product_ref[:, rows] = product

    run(inputs_ref[:, skipped:], use)


def ring_shape(rows, width):
    chunk = min(256, rows // 2)
    return min(6, rows // chunk), chunk, width


def first_product(inputs, weight):
    tokens, features = inputs.shape
    rows = weight.shape[0]
    width = features - 2 * BLOCK
    ring = ring_shape(rows, width)
    return pl.pallas_call(
        first_kernel,
        in_specs=[
            pl.BlockSpec(memory_space=pltpu.VMEM),
            pl.BlockSpec(memory_space=pl.ANY),
        ],
        out_specs=pl.BlockSpec(memory_space=pltpu.VMEM),
        out_shape=jax.ShapeDtypeStruct((tokens, rows), jnp.float32),
        scratch_shapes=[pltpu.VMEM(ring, jnp.bfloat16), pltpu.SemaphoreType.DMA((ring[0],))],
        compiler_params=pltpu.CompilerParams(vmem_limit_bytes=32 * 1024 * 1024),
        cost_estimate=pl.CostEstimate(
            flops=2 * tokens * rows * width, bytes_accessed=rows * width * 2, transcendentals=0
        ),
        name="first_product",
    )(inputs, weight)


def turn_kernel(scale, held_count, fill, where_ref, gathered_ref, weight_ref, panel_ref, aux_ref,
                *rest):
    if fill:
        out_ref, held_ref, held_sems = rest[0], rest[1], rest[-1]
        rest = rest[:-1]
    else:
        held_ref, out_ref = rest[0], rest[1 if held_count else 0]
    ring, panel, aux, wide, inputs, product, ring_sems, side_sems = rest[-8:]
    slots, chunk, width = ring.shape
    skipped = weight_ref.shape[1] - width
    streams = weight_ref.shape[0] // chunk - held_count
    ahead = min(2, held_count)

    def copy(index, slot):
        rows = pl.ds(pl.multiple_of((held_count + index) * chunk, chunk), chunk)
        return pltpu.make_async_copy(
            weight_ref.at[rows, pl.ds(skipped, width)], ring.at[slot], ring_sems.at[slot]
        )

    panel_copy = pltpu.make_async_copy(
        panel_ref.at[:, pl.ds(skipped, width)], panel, side_sems.at[0]
    )
    aux_copy = pltpu.make_async_copy(aux_ref, aux, side_sems.at[1])
    def held_copy(index):
        rows = pl.ds(pl.multiple_of(index * chunk, chunk), chunk)
        return pltpu.make_async_copy(
            weight_ref.at[rows, pl.ds(skipped, width)], held_ref.at[rows, :], held_sems.at[index]
        )

    if fill:
        for index in range(ahead):
            held_copy(index).start()
    panel_copy.start()
    aux_copy.start()
    for index in range(slots):
        copy(index, index).start()
    if fill:
        for index in range(ahead, held_count):
            held_copy(index).start()

    peers, own, _ = gathered_ref.shape
    for peer in range(peers):
        wide[peer * own : (peer + 1) * own, :] = gathered_ref[peer].astype(jnp.float32)
    inputs[...] = wide[...].astype(jnp.bfloat16)

    def place_of(index):
        return pl.multiple_of(index * chunk, chunk)

    def held_product(index):
        if fill:
            held_copy(index).wait()
        return nt_dot(inputs[:, skipped:], held_ref[pl.ds(place_of(index), chunk), :])

    for index in range(ahead):
        product[:, index * chunk : (index + 1) * chunk] = held_product(index)
    panel_copy.wait()
    panel_inputs = nt_dot(inputs[:, skipped:], panel[...])
    aux_copy.wait()
    rows = product.shape[1]
    tile = min(1024, rows)
    early = ahead * chunk
    for first in range(0, rows, tile):
        change = corrected(inputs[:, :skipped], panel_inputs, aux, slice(first, first + tile))
        both = min(max(early - first, 0), tile)
        if both:
            product[:, first : first + both] += change[:, :both]
        if both < tile:
            product[:, first + both : first + tile] = change[:, both:]

    def use(index, value):
        first = place_of(index)
        value = product[:, pl.ds(first, chunk)] + value
        hand_out(out_ref, value, inputs, where_ref, (first, chunk), scale)

    for index in range(ahead):
        value = product[:, index * chunk : (index + 1) * chunk]
        hand_out(out_ref, value, inputs, where_ref, (index * chunk, chunk), scale)

    def step(index, _):
        if held_count > ahead:
            @pl.when(index + ahead < held_count)
            def _():
                use(index + ahead, held_product(index + ahead))

        slot = lax.rem(index, slots)
        copy(index, slot).wait()
        use(held_count + index, nt_dot(inputs[:, skipped:], ring[slot]))

        @pl.when(index + slots < streams)
        def _():
            copy(index + slots, slot).start()

        return 0

    lax.fori_loop(0, streams, step, 0)


def turn_product(where, gathered_inputs, weight, panel, aux, held, held_count, scale, out_shape):
    peers, own, features = gathered_inputs.shape
    tokens = peers * own
    rows = weight.shape[0]
    count = 2 * BLOCK
    width = features - count
    chunk = min(256, rows // 2)
    fill = held is None and held_count > 0
    ring = (min(3 if held_count else 6, rows // chunk - held_count), chunk, width)
    vmem = pl.BlockSpec(memory_space=pltpu.VMEM)
    hbm = pl.BlockSpec(memory_space=pl.ANY)
    operands = [where, gathered_inputs, weight, panel, aux]
    if held is not None:
        operands.append(pltpu.with_memory_space_constraint(held, pltpu.VMEM))
    return pl.pallas_call(
        functools.partial(turn_kernel, scale, held_count, fill),
        in_specs=[pl.BlockSpec(memory_space=pltpu.SMEM), vmem, hbm, hbm, hbm] + [vmem] * (len(operands) - 5),
        out_specs=[vmem] * 2 if fill else vmem,
        out_shape=[out_shape, pltpu.VMEM((held_count * chunk, width), jnp.bfloat16)] if fill else out_shape,
        scratch_shapes=[
            pltpu.VMEM(ring, jnp.bfloat16),
            pltpu.VMEM((count, width), jnp.bfloat16),
            pltpu.VMEM(aux.shape, jnp.bfloat16),
            pltpu.VMEM((tokens, features), jnp.float32),
            pltpu.VMEM((tokens, features), jnp.bfloat16),
            pltpu.VMEM((tokens, rows), jnp.float32),
            pltpu.SemaphoreType.DMA((ring[0],)),
            pltpu.SemaphoreType.DMA((2,)),
        ] + [pltpu.SemaphoreType.DMA((held_count,))] * fill,
        compiler_params=pltpu.CompilerParams(vmem_limit_bytes=TURN_VMEM),
        cost_estimate=pl.CostEstimate(
            flops=2 * tokens * rows * features, bytes_accessed=rows * width * 2, transcendentals=0
        ),
        name="turn_product",
    )(*operands)


def per_device(tokens, up_weight, hess_panel, keep_mask):
    weight = up_weight[0]
    local_panel = hess_panel[0].astype(jnp.bfloat16)
    count = 2 * BLOCK
    features = weight.shape[1]
    scale = features ** (-0.5)
    row_size = lax.axis_size("row")
    own = tokens.shape[0]
    held = local_panel.shape[1]
    position = lax.axis_index("layer")
    depth = lax.axis_size("layer")
    start = lax.axis_index("row") * held

    width = min(count, held)
    share = count // row_size
    factor_share = local_panel[:, :width].reshape(row_size, share * width // count, count)
    cut = own * features // count
    token_share = jnp.broadcast_to(tokens.reshape(1, cut, count), (row_size, cut, count))
    first = lax.all_to_all(
        jnp.concatenate([token_share, factor_share], 1), "row", split_axis=0, concat_axis=0
    )
    first, local_panel = lax.optimization_barrier((first, local_panel))
    portion = first[:, :cut].reshape(row_size * own, features)
    full_panel = lax.all_gather(local_panel, "row", axis=1, tiled=True)

    owned = [first[o, cut:].reshape(share, width) for o in range(count // width)]
    column = lax.broadcasted_iota(jnp.int32, local_panel.shape, 1) + start
    remote = jnp.where(column < count, jnp.zeros_like(local_panel), local_panel)
    partial_sum = nt_dot(lax.dynamic_slice_in_dim(portion, start, held, 1), remote)
    shares = jnp.concatenate([jnp.concatenate(owned, 1), *split_halves(partial_sum)], 0)
    shares, portion = lax.optimization_barrier((shares, portion))
    second = gathered(shares, "row")
    factor = second[:, :share].reshape(count, count)
    sums = second[:, share:].astype(jnp.float32).reshape(row_size, 2, row_size * own, count)

    product = first_product(portion, weight)
    pruned, aux = eliminate(weight, factor, keep_mask[0])

    rows = weight.shape[0]
    from_row = lax.axis_index("row") * rows
    where = jnp.stack([from_row % features, (from_row < features).astype(jnp.int32)])
    held_count = rows // min(256, rows // 2) * HELD // 16
    held = None
    results = jnp.zeros_like(tokens)
    for turn in range(depth):
        last = turn + 1 == depth
        out_shape = jax.ShapeDtypeStruct(((1 if last else 2) * row_size, own, rows), jnp.bfloat16)
        if turn:
            units = turn_product(
                where, copies, weight, full_panel, aux, held, held_count, scale, out_shape
            )
            if held_count and held is None:
                units, held = units
        else:
            units = combine(where, product, portion, sums.sum(axis=(0, 1)), aux, scale, out_shape)
        if last:
            spread = lax.all_to_all(units, "row", split_axis=0, concat_axis=0)
        else:
            pair = [turn, turn + 1]
            others = [layer for layer in range(depth) if layer not in pair]
            groups = [
                [layer * row_size + peer for layer in layers for peer in range(row_size)]
                for layers in [pair] + [others[i : i + 2] for i in range(0, len(others), 2)]
            ]
            spread = lax.all_to_all(
                units, ("layer", "row"), split_axis=0, concat_axis=0, axis_index_groups=groups
            )
        copies, produced = fold(spread, row_size, features)
        results = jnp.where(position == turn, produced, results)
        if not last:
            copies = lax.all_to_all(copies, "row", split_axis=0, concat_axis=0)
    return (results[None], pruned[None])


def solution(mesh):
    in_specs = (
        P("row", None),
        P("layer", "row", None),
        P("layer", None, "row"),
        P("layer", "row", None),
    )
    out_specs = (P("layer", "row", None), P("layer", "row", None))
    return jax.shard_map(
        per_device, mesh=mesh, in_specs=in_specs, out_specs=out_specs, check_vma=False
    )
```

```python
import functools

import jax
import jax.numpy as jnp
from jax import lax
from jax.experimental import pallas as pl
from jax.experimental.pallas import tpu as pltpu
from jax.sharding import PartitionSpec as P

BLOCK = 128
SUB = 16
HELD = 6
ELIMINATE_VMEM = 40 * 1024 * 1024
TURN_VMEM = 34 * 1024 * 1024

epsilon = 1e-05


def gathered(array, axis):
    size = lax.axis_size(axis)
    copies = jnp.broadcast_to(array[None], (size,) + array.shape)
    return lax.all_to_all(copies, axis, split_axis=0, concat_axis=0)


def nt_dot(left, right):
    return lax.dot_general(
        left, right, (((1,), (1,)), ((), ())), preferred_element_type=jnp.float32
    )


def nn_dot(left, right):
    return jnp.dot(left, right, preferred_element_type=jnp.float32)


def split_halves(value):
    high = value.astype(jnp.bfloat16)
    low = (value - high.astype(jnp.float32)).astype(jnp.bfloat16)
    return high, low


def identity(count):
    row = lax.broadcasted_iota(jnp.int32, (count, count), 0)
    column = lax.broadcasted_iota(jnp.int32, (count, count), 1)
    return jnp.where(row == column, 1.0, 0.0).astype(jnp.bfloat16)


def eliminate_kernel(scale, given, where_ref, scalar_ref, inverse_ref, inner_ref, cross_ref, weight_ref,
                     mask_ref, product_ref, inputs_ref, panel_ref, pruned_ref, aux_ref, out_ref,
                     state, dropped, errors):
    count = 2 * BLOCK
    depth = count * 8
    sheets = state.shape[0] // depth
    lanes = sheets * 128
    spots = [(g, q, slice((g * sheets + q) * 128, (g * sheets + q + 1) * 128))
             for g in range(8) for q in range(sheets)]

    def place(g, q, first, size):
        return pl.ds(q * depth + first * 8 + g, size, stride=8)

    def plane(q, j):
        return slice(q * depth + j * 8, q * depth + (j + 1) * 8)

    eye = identity(count)
    columns = nt_dot(eye, weight_ref[...])
    drops = nt_dot(eye, (1 - mask_ref[...]).astype(jnp.float32).astype(jnp.bfloat16))
    for g, q, where in spots:
        state[place(g, q, 0, count), :] = columns[:, where]
        dropped[place(g, q, 0, count), :] = drops[:, where]

    def stacked(first, size):
        wide = jnp.concatenate([errors[place(g, q, first, size), :] for g, q, _ in spots], 1)
        return jnp.concatenate(split_halves(wide), 0)

    def subtract(product, first, size):
        for g, q, where in spots:
            at = place(g, q, first, size)
            state[at, :] = state[at, :] - product[:, where]

    for block in range(2):
        for part in range(BLOCK // SUB):
            first = block * BLOCK + part * SUB
            planes = [[state[plane(q, first + i), :] for q in range(sheets)] for i in range(SUB)]
            for i in range(SUB):
                j = first + i
                inverse = inverse_ref[j]
                error = []
                for q in range(sheets):
                    lost = planes[i][q] * dropped[plane(q, j), :]
                    error.append(lost * inverse)
                    state[plane(q, j), :] = planes[i][q] - lost
                    errors[plane(q, j), :] = error[q]
                for k in range(i + 1, SUB):
                    scalar = scalar_ref[j * SUB + k]
                    for q in range(sheets):
                        planes[k][q] = planes[k][q] - error[q] * scalar
            after = first + SUB
            left = (block + 1) * BLOCK - after
            if left:
                factor = inner_ref[block * (BLOCK // SUB) + part, after : after + left, :]
                subtract(nn_dot(factor, stacked(first, SUB)), after, left)
        if block == 0:
            subtract(nn_dot(cross_ref[...], stacked(0, BLOCK)), BLOCK, BLOCK)

    small = identity(128)
    for g, q, where in spots:
        kept = state[place(g, q, 0, count), :].astype(jnp.bfloat16)
        aux_ref[0:count, where] = kept
        aux_ref[count:, where] = errors[place(g, q, 0, count), :].astype(jnp.bfloat16)
        pruned_ref[where, :] = nt_dot(small, kept).astype(jnp.bfloat16)

    rows = min(given, weight_ref.shape[0])
    step = min(512, rows)
    base = pl.program_id(0) * weight_ref.shape[0]
    for first in range(0, rows, step):
        place = slice(first, first + step)
        change = corrected(inputs_ref[:, :count], panel_ref[...], aux_ref, place)
        value = product_ref[:, place] + change
        hand_out(out_ref, value, inputs_ref, where_ref, base, place, scale)


def eliminate(weight, factor, mask, where, product, inputs, panel_inputs, scale, copies):
    count = 2 * BLOCK
    given = weight.shape[0]
    rows = pl.cdiv(given, 1024) * 1024
    if rows != given:
        more = ((0, rows - given), (0, 0))
        weight, mask = jnp.pad(weight[:, :count], more), jnp.pad(mask, more)
    tile = 1024 if rows % 2048 else 2048
    subs = count // SUB
    wide = factor.astype(jnp.float32)
    row = lax.broadcasted_iota(jnp.int32, wide.shape, 0)
    column = lax.broadcasted_iota(jnp.int32, wide.shape, 1)
    inverse = 1.0 / jnp.sum(jnp.where(row == column, wide, 0.0), axis=1)
    near = jnp.where(row // SUB == column // SUB, wide, 0.0)
    scalars = near.reshape(count, subs, SUB).sum(axis=1).reshape(-1)
    columns = factor.T.reshape(count, subs, SUB).transpose(1, 0, 2)
    inner = jnp.concatenate([columns, columns], 2)
    cross = factor[:BLOCK, BLOCK:].T
    cross = jnp.concatenate([cross, cross], 1)
    smem = pl.BlockSpec(memory_space=pltpu.SMEM)
    tokens = inputs.shape[0]
    own = tokens // (copies // 2)
    part = min(given, tile)
    hbm = pltpu.MemorySpace.HBM
    pruned, aux, units = pl.pallas_call(
        functools.partial(eliminate_kernel, scale, given),
        grid=(rows // tile,),
        in_specs=[
            smem,
            smem,
            smem,
            pl.BlockSpec((subs, count, 2 * SUB), lambda i: (0, 0, 0)),
            pl.BlockSpec((BLOCK, count), lambda i: (0, 0)),
            pl.BlockSpec((tile, count), lambda i: (i, 0)),
            pl.BlockSpec((tile, count), lambda i: (i, 0)),
            pl.BlockSpec((tokens, part), lambda i: (0, i)),
            pl.BlockSpec(inputs.shape, lambda i: (0, 0)),
            pl.BlockSpec((tokens, count), lambda i: (0, 0)),
        ],
        out_specs=[
            pl.BlockSpec((tile, count), lambda i: (i, 0)),
            pl.BlockSpec((2 * count, tile), lambda i: (0, i)),
            pl.BlockSpec((copies, own, part), lambda i: (0, 0, i)),
        ],
        out_shape=[
            jax.ShapeDtypeStruct((rows, count), jnp.bfloat16),
            jax.ShapeDtypeStruct((2 * count, rows), jnp.bfloat16),
            jax.ShapeDtypeStruct((copies, own, given), jnp.bfloat16),
        ],
        scratch_shapes=[pltpu.VMEM((tile * count // 128, 128), jnp.float32)] * 3,
        compiler_params=pltpu.CompilerParams(vmem_limit_bytes=ELIMINATE_VMEM),
        cost_estimate=pl.CostEstimate(
            flops=2 * rows * count * count, bytes_accessed=rows * count * 12, transcendentals=0
        ),
        name="eliminate",
    )(
        where, scalars, inverse, inner, cross, weight,
        pltpu.with_memory_space_constraint(mask, hbm), product, inputs, panel_inputs,
    )
    return pruned[:given], aux[:, :given], units


def corrected(lead, panel_inputs, aux_ref, place):
    count = 2 * BLOCK
    tokens = lead.shape[0]
    both = nn_dot(jnp.concatenate(split_halves(panel_inputs), 0), aux_ref[count:, place])
    return nn_dot(lead, aux_ref[0:count, place]) - both[:tokens] - both[tokens:]


def hand_out(out_ref, value, inputs, where_ref, base, place, scale):
    units = (value * scale).astype(jnp.bfloat16).astype(jnp.float32)
    units = units / (1.0 + jnp.exp(-units))
    size = place.stop - place.start
    at = pl.ds(pl.multiple_of(where_ref[0] + base + place.start, 128), size)
    units = units + inputs[:, at].astype(jnp.float32) * where_ref[1].astype(jnp.float32)
    copies, own, _ = out_ref.shape
    peers = value.shape[0] // own
    for peer in range(peers):
        piece = units[peer * own : (peer + 1) * own].astype(jnp.bfloat16)
        for copy in range(peer, copies, peers):
            out_ref[copy, :, place] = piece


def fold_kernel(spread_ref, copies_ref, produced_ref):
    peers, own, features = copies_ref.shape
    rows = spread_ref.shape[2]
    parts = []
    for first in range(0, features, rows):
        part = None
        for peer in range(peers):
            if peer * rows % features == first:
                units = spread_ref[peer].astype(jnp.float32)
                part = units if part is None else part + units
        parts.append(part)
    combined = jnp.concatenate(parts, 1)
    moment = jnp.sum(combined * combined, axis=1, keepdims=True) * (1.0 / features)
    produced = (combined * lax.rsqrt(moment + epsilon)).astype(jnp.bfloat16)
    produced_ref[...] = produced
    for peer in range(peers):
        copies_ref[peer] = produced


def fold(spread, peers, features):
    own = spread.shape[1]
    return pl.pallas_call(
        fold_kernel,
        in_specs=[pl.BlockSpec(memory_space=pltpu.VMEM)],
        out_specs=[pl.BlockSpec(memory_space=pltpu.VMEM)] * 2,
        out_shape=[
            jax.ShapeDtypeStruct((peers, own, features), jnp.bfloat16),
            jax.ShapeDtypeStruct((own, features), jnp.bfloat16),
        ],
        compiler_params=pltpu.CompilerParams(vmem_limit_bytes=8 * 1024 * 1024),
        name="fold",
    )(spread)


def turned(inputs, columns):
    tokens = inputs.shape[0]
    more = (-tokens) % 128
    if more:
        inputs = jnp.concatenate([inputs, jnp.zeros((more, inputs.shape[1]), inputs.dtype)], 0)
    eye = identity(256)
    return [
        nt_dot(eye, inputs[:, at : at + 256]).astype(jnp.bfloat16)
        for at in range(columns, inputs.shape[1], 256)
    ]


def chunk_copy(weight_ref, target, sem, index, chunk):
    width = target.shape[-1]
    rows = pl.ds(pl.multiple_of(index * chunk, chunk), chunk)
    skipped = weight_ref.shape[1] - width
    return pltpu.make_async_copy(weight_ref.at[rows, pl.ds(skipped, width)], target, sem)


def stream(weight_ref, ring, ring_sems, right, product, held_count):
    slots, chunk, _ = ring.shape
    total = weight_ref.shape[0] // chunk - held_count
    pair = 2 if total % 2 == 0 and slots % 2 == 0 else 1

    def copy(index, slot):
        return chunk_copy(weight_ref, ring.at[slot], ring_sems.at[slot], held_count + index, chunk)

    def begin():
        for index in range(slots):
            copy(index, index).start()

    def step(i, _):
        index = i * pair
        slot = lax.rem(index, slots)
        for one in range(pair):
            copy(index + one, slot + one).wait()
        for one in range(pair):
            rows = pl.ds(pl.multiple_of((held_count + index + one) * chunk, chunk), chunk)
            product[rows, :] = nn_dot(ring[slot + one], right[...])

        @pl.when(index + slots < total)
        def _():
            for one in range(pair):
                copy(index + slots + one, slot + one).start()

        return 0

    def run():
        lax.fori_loop(0, total // pair, step, 0)

    return begin, run


def first_kernel(inputs_ref, weight_ref, product_ref, ring, right, product, ring_sems):
    skipped = weight_ref.shape[1] - ring.shape[2]
    begin, run = stream(weight_ref, ring, ring_sems, right, product, 0)
    begin()
    for i, part in enumerate(turned(inputs_ref[...], skipped)):
        right[i * 256 : (i + 1) * 256, :] = part
    run()
    rows = product.shape[0]
    step = min(512, rows)
    tokens = inputs_ref.shape[0]
    for first in range(0, rows, step):
        product_ref[:, first : first + step] = product[first : first + step, :].T[:tokens]


def padded(tokens):
    return pl.cdiv(tokens, 128) * 128


def first_product(inputs, weight):
    tokens, features = inputs.shape
    rows = weight.shape[0]
    width = features - 2 * BLOCK
    chunk = min(256, rows // 2)
    ring = (min(6, rows // chunk), chunk, width)
    return pl.pallas_call(
        first_kernel,
        in_specs=[
            pl.BlockSpec(memory_space=pltpu.VMEM),
            pl.BlockSpec(memory_space=pl.ANY),
        ],
        out_specs=pl.BlockSpec(memory_space=pltpu.VMEM),
        out_shape=jax.ShapeDtypeStruct((tokens, rows), jnp.float32),
        scratch_shapes=[
            pltpu.VMEM(ring, jnp.bfloat16),
            pltpu.VMEM((width, padded(tokens)), jnp.bfloat16),
            pltpu.VMEM((rows, padded(tokens)), jnp.float32),
            pltpu.SemaphoreType.DMA((ring[0],)),
        ],
        compiler_params=pltpu.CompilerParams(vmem_limit_bytes=40 * 1024 * 1024),
        cost_estimate=pl.CostEstimate(
            flops=2 * tokens * rows * width, bytes_accessed=rows * width * 2, transcendentals=0
        ),
        name="first_product",
    )(inputs, weight)


def turn_kernel(scale, held_count, fill, where_ref, gathered_ref, weight_ref, panel_ref, aux_ref,
                *rest):
    if fill:
        out_ref, held_ref, held_sems = rest[0], rest[1], rest[-1]
        rest = rest[:-1]
    else:
        held_ref, out_ref = rest[0], rest[1 if held_count else 0]
    ring, panel, aux, wide, inputs, right, product, ring_sems, side_sems = rest[-9:]
    slots, chunk, width = ring.shape
    skipped = weight_ref.shape[1] - width
    begin, run = stream(weight_ref, ring, ring_sems, right, product, held_count)
    panel_copy = pltpu.make_async_copy(
        panel_ref.at[:, pl.ds(skipped, width)], panel, side_sems.at[0]
    )
    aux_copy = pltpu.make_async_copy(aux_ref, aux, side_sems.at[1])

    def held_copy(index):
        rows = pl.ds(pl.multiple_of(index * chunk, chunk), chunk)
        return chunk_copy(weight_ref, held_ref.at[rows, :], held_sems.at[index], index, chunk)

    if fill:
        for index in range(held_count):
            held_copy(index).start()
    begin()
    panel_copy.start()
    aux_copy.start()

    peers, own, _ = gathered_ref.shape
    for peer in range(peers):
        wide[peer * own : (peer + 1) * own, :] = gathered_ref[peer].astype(jnp.float32)
    inputs[...] = wide[...].astype(jnp.bfloat16)
    for i, part in enumerate(turned(inputs[...], skipped)):
        right[i * 256 : (i + 1) * 256, :] = part

    pair = 2 if held_count % 2 == 0 else 1

    def held_step(i, _):
        for one in range(pair):
            if fill:
                held_copy(i * pair + one).wait()
        for one in range(pair):
            rows = pl.ds(pl.multiple_of((i * pair + one) * chunk, chunk), chunk)
            product[rows, :] = nn_dot(held_ref[rows, :], right[...])
        return 0

    if held_count:
        lax.fori_loop(0, held_count // pair, held_step, 0)
    run()

    panel_copy.wait()
    tokens = peers * own
    panel_inputs = nn_dot(panel[...], right[...]).T[:tokens]
    aux_copy.wait()
    rows = product.shape[0]
    step = min(512, rows)
    for first in range(0, rows, step):
        place = slice(first, first + step)
        change = corrected(inputs[:, :skipped], panel_inputs, aux, place)
        value = product[place, :].T[:tokens] + change
        hand_out(out_ref, value, inputs, where_ref, 0, place, scale)


def turn_product(where, gathered_inputs, weight, panel, aux, held, held_count, scale, out_shape):
    peers, own, features = gathered_inputs.shape
    tokens = peers * own
    rows = weight.shape[0]
    count = 2 * BLOCK
    width = features - count
    chunk = min(256, rows // 2)
    fill = held is None and held_count > 0
    ring = (min(4, rows // chunk - held_count), chunk, width)
    vmem = pl.BlockSpec(memory_space=pltpu.VMEM)
    hbm = pl.BlockSpec(memory_space=pltpu.MemorySpace.HBM)
    operands = [where, gathered_inputs, weight, panel, aux]
    if held is not None:
        operands.append(pltpu.with_memory_space_constraint(held, pltpu.VMEM))
    return pl.pallas_call(
        functools.partial(turn_kernel, scale, held_count, fill),
        in_specs=[pl.BlockSpec(memory_space=pltpu.SMEM), vmem, hbm, hbm, hbm] + [vmem] * (len(operands) - 5),
        out_specs=[vmem] * 2 if fill else vmem,
        out_shape=[out_shape, pltpu.VMEM((held_count * chunk, width), jnp.bfloat16)] if fill else out_shape,
        scratch_shapes=[
            pltpu.VMEM(ring, jnp.bfloat16),
            pltpu.VMEM((count, width), jnp.bfloat16),
            pltpu.VMEM(aux.shape, jnp.bfloat16),
            pltpu.VMEM((tokens, features), jnp.float32),
            pltpu.VMEM((tokens, features), jnp.bfloat16),
            pltpu.VMEM((width, padded(tokens)), jnp.bfloat16),
            pltpu.VMEM((rows, padded(tokens)), jnp.float32),
            pltpu.SemaphoreType.DMA((ring[0],)),
            pltpu.SemaphoreType.DMA((2,)),
        ] + [pltpu.SemaphoreType.DMA((held_count,))] * fill,
        compiler_params=pltpu.CompilerParams(vmem_limit_bytes=TURN_VMEM),
        cost_estimate=pl.CostEstimate(
            flops=2 * tokens * rows * features, bytes_accessed=rows * width * 2, transcendentals=0
        ),
        name="turn_product",
    )(*operands)


def per_device(tokens, up_weight, hess_panel, keep_mask):
    weight = up_weight[0]
    local_panel = hess_panel[0].astype(jnp.bfloat16)
    count = 2 * BLOCK
    features = weight.shape[1]
    scale = features ** (-0.5)
    row_size = lax.axis_size("row")
    own = tokens.shape[0]
    held = local_panel.shape[1]
    position = lax.axis_index("layer")
    depth = lax.axis_size("layer")
    start = lax.axis_index("row") * held

    width = min(count, held)
    share = count // row_size
    factor_share = local_panel[:, :width].reshape(row_size, share * width // count, count)
    cut = own * features // count
    token_share = jnp.broadcast_to(tokens.reshape(1, cut, count), (row_size, cut, count))
    first = lax.all_to_all(
        jnp.concatenate([token_share, factor_share], 1), "row", split_axis=0, concat_axis=0
    )
    first, local_panel = lax.optimization_barrier((first, local_panel))
    portion = first[:, :cut].reshape(row_size * own, features)
    full_panel = lax.all_gather(local_panel, "row", axis=1, tiled=True)

    owned = [first[o, cut:].reshape(share, width) for o in range(count // width)]
    column = lax.broadcasted_iota(jnp.int32, local_panel.shape, 1) + start
    remote = jnp.where(column < count, jnp.zeros_like(local_panel), local_panel)
    partial_sum = nt_dot(lax.dynamic_slice_in_dim(portion, start, held, 1), remote)
    shares = jnp.concatenate([jnp.concatenate(owned, 1), *split_halves(partial_sum)], 0)
    shares, portion = lax.optimization_barrier((shares, portion))
    second = gathered(shares, "row")
    factor = second[:, :share].reshape(count, count)
    sums = second[:, share:].astype(jnp.float32).reshape(row_size, 2, row_size * own, count)

    product = first_product(portion, weight)
    rows = weight.shape[0]
    from_row = lax.axis_index("row") * rows
    where = jnp.stack([from_row % features, (from_row < features).astype(jnp.int32)])
    pruned, aux, units = eliminate(
        weight, factor, keep_mask[0], where, product, portion, sums.sum(axis=(0, 1)), scale, 2 * row_size
    )
    held_count = rows // min(256, rows // 2) * HELD // 16
    held = None
    results = jnp.zeros_like(tokens)
    for turn in range(depth):
        last = turn + 1 == depth
        if turn:
            out_shape = jax.ShapeDtypeStruct(((1 if last else 2) * row_size, own, rows), jnp.bfloat16)
            units = turn_product(
                where, copies, weight, full_panel, aux, held, held_count, scale, out_shape
            )
            if held_count and held is None:
                units, held = units
        if last:
            spread = lax.all_to_all(units, "row", split_axis=0, concat_axis=0)
        else:
            pair = [turn, turn + 1]
            others = [layer for layer in range(depth) if layer not in pair]
            groups = [
                [layer * row_size + peer for layer in layers for peer in range(row_size)]
                for layers in [pair] + [others[i : i + 2] for i in range(0, len(others), 2)]
            ]
            spread = lax.all_to_all(
                units, ("layer", "row"), split_axis=0, concat_axis=0, axis_index_groups=groups
            )
        copies, produced = fold(spread, row_size, features)
        results = jnp.where(position == turn, produced, results)
        if not last:
            copies = lax.all_to_all(copies, "row", split_axis=0, concat_axis=0)
    return (results[None], pruned[None])


def solution(mesh):
    in_specs = (
        P("row", None),
        P("layer", "row", None),
        P("layer", None, "row"),
        P("layer", "row", None),
    )
    out_specs = (P("layer", "row", None), P("layer", "row", None))
    return jax.shard_map(
        per_device, mesh=mesh, in_specs=in_specs, out_specs=out_specs, check_vma=False
    )
```

```python
import functools

import jax
import jax.numpy as jnp
from jax import lax
from jax.experimental import pallas as pl
from jax.experimental.pallas import tpu as pltpu
from jax.sharding import PartitionSpec as P

BLOCK = 128
SUB = 16
ELIMINATE_VMEM = 46 * 1024 * 1024
TURN_VMEM = 36 * 1024 * 1024

epsilon = 1e-05


def gathered(array, axis):
    size = lax.axis_size(axis)
    copies = jnp.broadcast_to(array[None], (size,) + array.shape)
    return lax.all_to_all(copies, axis, split_axis=0, concat_axis=0)


def nt_dot(left, right):
    return lax.dot_general(
        left, right, (((1,), (1,)), ((), ())), preferred_element_type=jnp.float32
    )


def nn_dot(left, right):
    return jnp.dot(left, right, preferred_element_type=jnp.float32)


def split_halves(value):
    high = value.astype(jnp.bfloat16)
    low = (value - high.astype(jnp.float32)).astype(jnp.bfloat16)
    return high, low


def identity(count):
    row = lax.broadcasted_iota(jnp.int32, (count, count), 0)
    column = lax.broadcasted_iota(jnp.int32, (count, count), 1)
    return jnp.where(row == column, 1.0, 0.0).astype(jnp.bfloat16)


def eliminate_kernel(scale, part_rows, where_ref, scalar_ref, inverse_ref, inner_ref, cross_ref, weight_ref,
                     mask_ref, product_ref, inputs_ref, panel_ref, whole_ref, pruned_ref, aux_ref, out_ref,
                     state, dropped, errors, ring, own_product, sems):
    count = 2 * BLOCK
    depth = count * 8
    sheets = state.shape[0] // depth
    lanes = sheets * 128
    spots = [(g, q, slice((g * sheets + q) * 128, (g * sheets + q + 1) * 128))
             for g in range(8) for q in range(sheets)]

    def place(g, q, first, size):
        return pl.ds(q * depth + first * 8 + g, size, stride=8)

    def plane(q, j):
        return slice(q * depth + j * 8, q * depth + (j + 1) * 8)

    tile_index = pl.program_id(0)
    slots, chunk, _ = ring.shape

    def fetch(tile, slot):
        row = pl.multiple_of(tile * part_rows + part_rows // 2 + slot * chunk, chunk)
        return chunk_copy(whole_ref, ring.at[slot], sems.at[slot], row)

    @pl.when(tile_index == 0)
    def _():
        for slot in range(slots):
            fetch(0, slot).start()

    def multiply(slot):
        fetch(tile_index, slot).wait()
        own_product[:, slot * chunk : (slot + 1) * chunk] = nt_dot(inputs_ref[:, count:], ring[slot])

    def renew(slot):
        @pl.when(tile_index + 1 < pl.num_programs(0))
        def _():
            fetch(tile_index + 1, slot).start()

    eye = identity(count)
    columns = nt_dot(eye, weight_ref[...])
    drops = nt_dot(eye, (1 - mask_ref[...]).astype(jnp.float32).astype(jnp.bfloat16))
    for g, q, where in spots:
        state[place(g, q, 0, count), :] = columns[:, where]
        dropped[place(g, q, 0, count), :] = drops[:, where]

    def stacked(first, size):
        wide = jnp.concatenate([errors[place(g, q, first, size), :] for g, q, _ in spots], 1)
        return jnp.concatenate(split_halves(wide), 0)

    def subtract(product, first, size):
        for g, q, where in spots:
            at = place(g, q, first, size)
            state[at, :] = state[at, :] - product[:, where]

    for block in range(2):
        for part in range(BLOCK // SUB):
            first = block * BLOCK + part * SUB
            spread = 2 * (BLOCK // SUB) // slots
            slot, at_slot = divmod(block * (BLOCK // SUB) + part, spread)
            if at_slot == spread // 2:
                multiply(slot)
            planes = [[state[plane(q, first + i), :] for q in range(sheets)] for i in range(SUB)]
            for i in range(SUB):
                j = first + i
                inverse = inverse_ref[j]
                error = []
                for q in range(sheets):
                    lost = planes[i][q] * dropped[plane(q, j), :]
                    error.append(lost * inverse)
                    state[plane(q, j), :] = planes[i][q] - lost
                    errors[plane(q, j), :] = error[q]
                for k in range(i + 1, SUB):
                    scalar = scalar_ref[j * SUB + k]
                    for q in range(sheets):
                        planes[k][q] = planes[k][q] - error[q] * scalar
            after = first + SUB
            left = (block + 1) * BLOCK - after
            if left:
                factor = inner_ref[block * (BLOCK // SUB) + part, after : after + left, :]
                subtract(nn_dot(factor, stacked(first, SUB)), after, left)
            if at_slot == spread - 1:
                renew(slot)
        if block == 0:
            subtract(nn_dot(cross_ref[...], stacked(0, BLOCK)), BLOCK, BLOCK)

    small = identity(128)
    for g, q, where in spots:
        kept = state[place(g, q, 0, count), :].astype(jnp.bfloat16)
        aux_ref[0:count, where] = kept
        aux_ref[count:, where] = errors[place(g, q, 0, count), :].astype(jnp.bfloat16)
        pruned_ref[where, :] = nt_dot(small, kept).astype(jnp.bfloat16)

    half = part_rows // 2
    step = min(512, half)
    for first in range(0, part_rows, step):
        place = slice(first, first + step)
        change = corrected(inputs_ref[:, :count], panel_ref[...], aux_ref, place)
        source, at = (product_ref, first) if first < half else (own_product, first - half)
        value = source[:, at : at + step] + change
        base = tile_index * part_rows + first
        out_ref[:, place] = units_of(value, inputs_ref, where_ref, base, scale)


def tile_rows(given):
    return 2048 if given % 2048 == 0 else 1024


def eliminate(weight, factor, mask, where, product, inputs, panel_inputs, scale):
    count = 2 * BLOCK
    given = weight.shape[0]
    whole = weight
    rows = pl.cdiv(given, 1024) * 1024
    if rows != given:
        more = ((0, rows - given), (0, 0))
        weight, mask = jnp.pad(weight[:, :count], more), jnp.pad(mask, more)
    tile = tile_rows(given)
    subs = count // SUB
    wide = factor.astype(jnp.float32)
    row = lax.broadcasted_iota(jnp.int32, wide.shape, 0)
    column = lax.broadcasted_iota(jnp.int32, wide.shape, 1)
    inverse = 1.0 / jnp.sum(jnp.where(row == column, wide, 0.0), axis=1)
    near = jnp.where(row // SUB == column // SUB, wide, 0.0)
    scalars = near.reshape(count, subs, SUB).sum(axis=1).reshape(-1)
    columns = factor.T.reshape(count, subs, SUB).transpose(1, 0, 2)
    inner = jnp.concatenate([columns, columns], 2)
    cross = factor[:BLOCK, BLOCK:].T
    cross = jnp.concatenate([cross, cross], 1)
    smem = pl.BlockSpec(memory_space=pltpu.SMEM)
    tokens = inputs.shape[0]
    part = min(given, tile)
    chunk = min(256, part // 2)
    slots = part // 2 // chunk
    hbm = pltpu.MemorySpace.HBM
    pruned, aux, units = pl.pallas_call(
        functools.partial(eliminate_kernel, scale, part),
        grid=(rows // tile,),
        in_specs=[
            smem,
            smem,
            smem,
            pl.BlockSpec((subs, count, 2 * SUB), lambda i: (0, 0, 0)),
            pl.BlockSpec((BLOCK, count), lambda i: (0, 0)),
            pl.BlockSpec((tile, count), lambda i: (i, 0)),
            pl.BlockSpec((tile, count), lambda i: (i, 0)),
            pl.BlockSpec((tokens, part // 2), lambda i: (0, i)),
            pl.BlockSpec(inputs.shape, lambda i: (0, 0)),
            pl.BlockSpec((tokens, count), lambda i: (0, 0)),
            pl.BlockSpec(memory_space=hbm),
        ],
        out_specs=[
            pl.BlockSpec((tile, count), lambda i: (i, 0)),
            pl.BlockSpec((2 * count, tile), lambda i: (0, i)),
            pl.BlockSpec((tokens, part), lambda i: (0, i)),
        ],
        out_shape=[
            jax.ShapeDtypeStruct((rows, count), jnp.bfloat16),
            hbm((2 * count, rows), jnp.bfloat16),
            jax.ShapeDtypeStruct((tokens, given), jnp.bfloat16),
        ],
        scratch_shapes=[pltpu.VMEM((tile * count // 128, 128), jnp.float32)] * 3 + [
            pltpu.VMEM((slots, chunk, inputs.shape[1] - count), jnp.bfloat16),
            pltpu.VMEM((tokens, part // 2), jnp.float32),
            pltpu.SemaphoreType.DMA((slots,)),
        ],
        compiler_params=pltpu.CompilerParams(vmem_limit_bytes=ELIMINATE_VMEM),
        cost_estimate=pl.CostEstimate(
            flops=2 * rows * count * count, bytes_accessed=rows * count * 12, transcendentals=0
        ),
        name="eliminate",
    )(
        where, scalars, inverse, inner, cross, weight,
        pltpu.with_memory_space_constraint(mask, hbm), product, inputs, panel_inputs, whole,
    )
    return pruned[:given], aux[:, :given], units


def corrected(lead, panel_inputs, aux_ref, place):
    count = 2 * BLOCK
    tokens = lead.shape[0]
    both = nn_dot(jnp.concatenate(split_halves(panel_inputs), 0), aux_ref[count:, place])
    return nn_dot(lead, aux_ref[0:count, place]) - both[:tokens] - both[tokens:]


def units_of(value, inputs, where_ref, first, scale):
    units = (value * scale).astype(jnp.bfloat16).astype(jnp.float32)
    units = units / (1.0 + jnp.exp(-units))
    at = pl.ds(pl.multiple_of(where_ref[0] + first, 128), value.shape[1])
    units = units + inputs[:, at].astype(jnp.float32) * where_ref[1].astype(jnp.float32)
    return units.astype(jnp.bfloat16)


def fold_kernel(spread_ref, copies_ref, produced_ref):
    peers, own, features = copies_ref.shape
    rows = spread_ref.shape[2]
    parts = []
    for first in range(0, features, rows):
        part = None
        for peer in range(peers):
            if peer * rows % features == first:
                units = spread_ref[peer].astype(jnp.float32)
                part = units if part is None else part + units
        parts.append(part)
    combined = jnp.concatenate(parts, 1)
    moment = jnp.sum(combined * combined, axis=1, keepdims=True) * (1.0 / features)
    produced = (combined * lax.rsqrt(moment + epsilon)).astype(jnp.bfloat16)
    produced_ref[...] = produced
    for peer in range(peers):
        copies_ref[peer] = produced


def fold(spread, peers, features):
    own = spread.shape[1]
    return pl.pallas_call(
        fold_kernel,
        in_specs=[pl.BlockSpec(memory_space=pltpu.VMEM)],
        out_specs=[pl.BlockSpec(memory_space=pltpu.VMEM)] * 2,
        out_shape=[
            jax.ShapeDtypeStruct((peers, own, features), jnp.bfloat16),
            jax.ShapeDtypeStruct((own, features), jnp.bfloat16),
        ],
        compiler_params=pltpu.CompilerParams(vmem_limit_bytes=8 * 1024 * 1024),
        name="fold",
    )(spread)


def chunk_copy(weight_ref, target, sem, row):
    chunk, width = target.shape
    skipped = weight_ref.shape[1] - width
    return pltpu.make_async_copy(
        weight_ref.at[pl.ds(row, chunk), pl.ds(skipped, width)], target, sem
    )


def stream(weight_ref, ring, ring_sems, total, row_of, inputs, use):
    slots = ring.shape[0]

    def copy(index, slot):
        return chunk_copy(weight_ref, ring.at[slot], ring_sems.at[slot], row_of(index))

    def begin():
        for index in range(slots):
            copy(index, index).start()

    def step(index, _):
        slot = lax.rem(index, slots)
        copy(index, slot).wait()
        use(index, nt_dot(inputs(), ring[slot]))

        @pl.when(index + slots < total)
        def _():
            copy(index + slots, slot).start()

        return 0

    def run():
        lax.fori_loop(0, total, step, 0)

    return begin, run


def first_kernel(part_rows, inputs_ref, weight_ref, product_ref, ring, ring_sems):
    chunk, width = ring.shape[1:]
    skipped = weight_ref.shape[1] - width
    each = part_rows // 2 // chunk

    def row_of(index):
        return pl.multiple_of(index // each * part_rows + index % each * chunk, chunk)

    def use(index, product):
        product_ref[:, pl.ds(pl.multiple_of(index * chunk, chunk), chunk)] = product

    total = product_ref.shape[1] // chunk
    begin, run = stream(
        weight_ref, ring, ring_sems, total, row_of, lambda: inputs_ref[:, skipped:], use
    )
    begin()
    run()


def first_product(inputs, weight):
    tokens, features = inputs.shape
    rows = weight.shape[0]
    width = features - 2 * BLOCK
    part = min(rows, tile_rows(rows))
    chunk = min(256, part // 2)
    ring = (min(6, rows // 2 // chunk), chunk, width)
    return pl.pallas_call(
        functools.partial(first_kernel, part),
        in_specs=[
            pl.BlockSpec(memory_space=pltpu.VMEM),
            pl.BlockSpec(memory_space=pltpu.MemorySpace.HBM),
        ],
        out_specs=pl.BlockSpec(memory_space=pltpu.VMEM),
        out_shape=jax.ShapeDtypeStruct((tokens, rows // 2), jnp.float32),
        scratch_shapes=[pltpu.VMEM(ring, jnp.bfloat16), pltpu.SemaphoreType.DMA((ring[0],))],
        compiler_params=pltpu.CompilerParams(vmem_limit_bytes=32 * 1024 * 1024),
        cost_estimate=pl.CostEstimate(
            flops=tokens * rows * width, bytes_accessed=rows * width, transcendentals=0
        ),
        name="first_product",
    )(inputs, weight)


def turn_kernel(scale, where_ref, inputs_ref, weight_ref, panel_ref, aux_ref, out_ref, ring, panel,
                aux, change, ring_sems, side_sems):
    chunk, width = ring.shape[1:]
    skipped = weight_ref.shape[1] - width

    def place_of(index):
        return pl.multiple_of(index * chunk, chunk)

    def use(index, product):
        place = pl.ds(place_of(index), chunk)
        value = product + change[:, place]
        out_ref[:, place] = units_of(value, inputs_ref, where_ref, place_of(index), scale)

    rows = change.shape[1]
    begin, run = stream(
        weight_ref, ring, ring_sems, rows // chunk, place_of, lambda: inputs_ref[:, skipped:], use
    )
    panel_copy = pltpu.make_async_copy(
        panel_ref.at[:, pl.ds(skipped, width)], panel, side_sems.at[0]
    )
    aux_copy = pltpu.make_async_copy(aux_ref, aux, side_sems.at[1])
    panel_copy.start()
    aux_copy.start()
    begin()
    panel_copy.wait()
    panel_inputs = nt_dot(inputs_ref[:, skipped:], panel[...])
    aux_copy.wait()
    step = min(1024, rows)
    for first in range(0, rows, step):
        place = slice(first, first + step)
        change[:, place] = corrected(inputs_ref[:, :skipped], panel_inputs, aux, place)
    run()


def turn_product(where, inputs, weight, panel, aux, scale):
    tokens, features = inputs.shape
    rows = weight.shape[0]
    count = 2 * BLOCK
    width = features - count
    chunk = min(256, rows // 2)
    ring = (min(6, rows // chunk), chunk, width)
    vmem = pl.BlockSpec(memory_space=pltpu.VMEM)
    hbm = pl.BlockSpec(memory_space=pltpu.MemorySpace.HBM)
    return pl.pallas_call(
        functools.partial(turn_kernel, scale),
        in_specs=[pl.BlockSpec(memory_space=pltpu.SMEM), vmem, hbm, hbm, hbm],
        out_specs=vmem,
        out_shape=jax.ShapeDtypeStruct((tokens, rows), jnp.bfloat16),
        scratch_shapes=[
            pltpu.VMEM(ring, jnp.bfloat16),
            pltpu.VMEM((count, width), jnp.bfloat16),
            pltpu.VMEM(aux.shape, jnp.bfloat16),
            pltpu.VMEM((tokens, rows), jnp.float32),
            pltpu.SemaphoreType.DMA((ring[0],)),
            pltpu.SemaphoreType.DMA((2,)),
        ],
        compiler_params=pltpu.CompilerParams(vmem_limit_bytes=TURN_VMEM),
        cost_estimate=pl.CostEstimate(
            flops=2 * tokens * rows * features, bytes_accessed=rows * width * 2, transcendentals=0
        ),
        name="turn_product",
    )(where, inputs, weight, panel, aux)


def per_device(tokens, up_weight, hess_panel, keep_mask):
    weight = up_weight[0]
    local_panel = hess_panel[0].astype(jnp.bfloat16)
    count = 2 * BLOCK
    features = weight.shape[1]
    scale = features ** (-0.5)
    row_size = lax.axis_size("row")
    own = tokens.shape[0]
    held = local_panel.shape[1]
    position = lax.axis_index("layer")
    depth = lax.axis_size("layer")
    start = lax.axis_index("row") * held

    width = min(count, held)
    share = count // row_size
    factor_share = local_panel[:, :width].reshape(row_size, share * width // count, count)
    cut = own * features // count
    token_share = jnp.broadcast_to(tokens.reshape(1, cut, count), (row_size, cut, count))
    first = lax.all_to_all(
        jnp.concatenate([token_share, factor_share], 1), "row", split_axis=0, concat_axis=0
    )
    first, local_panel = lax.optimization_barrier((first, local_panel))
    portion = first[:, :cut].reshape(row_size * own, features)
    full_panel = lax.all_gather(local_panel, "row", axis=1, tiled=True)

    owned = [first[o, cut:].reshape(share, width) for o in range(count // width)]
    column = lax.broadcasted_iota(jnp.int32, local_panel.shape, 1) + start
    remote = jnp.where(column < count, jnp.zeros_like(local_panel), local_panel)
    partial_sum = nt_dot(lax.dynamic_slice_in_dim(portion, start, held, 1), remote)
    shares = jnp.concatenate([jnp.concatenate(owned, 1), *split_halves(partial_sum)], 0)
    shares, portion = lax.optimization_barrier((shares, portion))
    second = gathered(shares, "row")
    factor = second[:, :share].reshape(count, count)
    sums = second[:, share:].astype(jnp.float32).reshape(row_size, 2, row_size * own, count)

    product = first_product(portion, weight)
    rows = weight.shape[0]
    from_row = lax.axis_index("row") * rows
    where = jnp.stack([from_row % features, (from_row < features).astype(jnp.int32)])
    pruned, aux, units = eliminate(
        weight, factor, keep_mask[0], where, product, portion, sums.sum(axis=(0, 1)), scale
    )
    results = jnp.zeros_like(tokens)
    for turn in range(depth):
        last = turn + 1 == depth
        if turn:
            portion = copies.reshape(row_size * own, features)
            units = turn_product(where, portion, weight, full_panel, aux, scale)
        units = units.reshape(row_size, own, rows)
        if last:
            spread = lax.all_to_all(units, "row", split_axis=0, concat_axis=0)
        else:
            pair = [turn, turn + 1]
            others = [layer for layer in range(depth) if layer not in pair]
            groups = [
                [layer * row_size + peer for layer in layers for peer in range(row_size)]
                for layers in [pair] + [others[i : i + 2] for i in range(0, len(others), 2)]
            ]
            spread = lax.all_to_all(
                jnp.concatenate([units, units], 0), ("layer", "row"), split_axis=0, concat_axis=0, axis_index_groups=groups
            )
        copies, produced = fold(spread, row_size, features)
        results = jnp.where(position == turn, produced, results)
        if not last:
            copies = lax.all_to_all(copies, "row", split_axis=0, concat_axis=0)
    return (results[None], pruned[None])


def solution(mesh):
    in_specs = (
        P("row", None),
        P("layer", "row", None),
        P("layer", None, "row"),
        P("layer", "row", None),
    )
    out_specs = (P("layer", "row", None), P("layer", "row", None))
    return jax.shard_map(
        per_device, mesh=mesh, in_specs=in_specs, out_specs=out_specs, check_vma=False
    )
```

```python
import functools

import jax
import jax.numpy as jnp
from jax import lax
from jax.experimental import pallas as pl
from jax.experimental.pallas import tpu as pltpu
from jax.sharding import PartitionSpec as P

BLOCK = 128
SUB = 16
ELIMINATE_VMEM = 40 * 1024 * 1024
TURN_VMEM = 36 * 1024 * 1024

epsilon = 1e-05


def gathered(array, axis):
    size = lax.axis_size(axis)
    copies = jnp.broadcast_to(array[None], (size,) + array.shape)
    return lax.all_to_all(copies, axis, split_axis=0, concat_axis=0)


def nt_dot(left, right):
    return lax.dot_general(
        left, right, (((1,), (1,)), ((), ())), preferred_element_type=jnp.float32
    )


def nn_dot(left, right):
    return jnp.dot(left, right, preferred_element_type=jnp.float32)


def split_halves(value):
    high = value.astype(jnp.bfloat16)
    low = (value - high.astype(jnp.float32)).astype(jnp.bfloat16)
    return high, low


def identity(count):
    row = lax.broadcasted_iota(jnp.int32, (count, count), 0)
    column = lax.broadcasted_iota(jnp.int32, (count, count), 1)
    return jnp.where(row == column, 1.0, 0.0).astype(jnp.bfloat16)


def eliminate_kernel(scale, part_rows, where_ref, scalar_ref, inverse_ref, inner_ref, cross_ref, weight_ref,
                     mask_ref, product_ref, inputs_ref, panel_ref, pruned_ref, aux_ref, out_ref,
                     state, dropped, errors):
    count = 2 * BLOCK
    depth = count * 8
    sheets = state.shape[0] // depth
    lanes = sheets * 128
    spots = [(g, q, slice((g * sheets + q) * 128, (g * sheets + q + 1) * 128))
             for g in range(8) for q in range(sheets)]

    def place(g, q, first, size):
        return pl.ds(q * depth + first * 8 + g, size, stride=8)

    def plane(q, j):
        return slice(q * depth + j * 8, q * depth + (j + 1) * 8)

    eye = identity(count)
    columns = nt_dot(eye, weight_ref[...])
    drops = nt_dot(eye, (1 - mask_ref[...]).astype(jnp.float32).astype(jnp.bfloat16))
    for g, q, where in spots:
        state[place(g, q, 0, count), :] = columns[:, where]
        dropped[place(g, q, 0, count), :] = drops[:, where]

    def stacked(first, size):
        wide = jnp.concatenate([errors[place(g, q, first, size), :] for g, q, _ in spots], 1)
        return jnp.concatenate(split_halves(wide), 0)

    def subtract(product, first, size):
        for g, q, where in spots:
            at = place(g, q, first, size)
            state[at, :] = state[at, :] - product[:, where]

    for block in range(2):
        for part in range(BLOCK // SUB):
            first = block * BLOCK + part * SUB
            planes = [[state[plane(q, first + i), :] for q in range(sheets)] for i in range(SUB)]
            for i in range(SUB):
                j = first + i
                inverse = inverse_ref[j]
                error = []
                for q in range(sheets):
                    lost = planes[i][q] * dropped[plane(q, j), :]
                    error.append(lost * inverse)
                    state[plane(q, j), :] = planes[i][q] - lost
                    errors[plane(q, j), :] = error[q]
                for k in range(i + 1, SUB):
                    scalar = scalar_ref[j * SUB + k]
                    for q in range(sheets):
                        planes[k][q] = planes[k][q] - error[q] * scalar
            after = first + SUB
            left = (block + 1) * BLOCK - after
            if left:
                factor = inner_ref[block * (BLOCK // SUB) + part, after : after + left, :]
                subtract(nn_dot(factor, stacked(first, SUB)), after, left)
        if block == 0:
            subtract(nn_dot(cross_ref[...], stacked(0, BLOCK)), BLOCK, BLOCK)

    small = identity(128)
    for g, q, where in spots:
        kept = state[place(g, q, 0, count), :].astype(jnp.bfloat16)
        aux_ref[0:count, where] = kept
        aux_ref[count:, where] = errors[place(g, q, 0, count), :].astype(jnp.bfloat16)
        pruned_ref[where, :] = nt_dot(small, kept).astype(jnp.bfloat16)

    step = min(512, part_rows)
    for first in range(0, part_rows, step):
        place = slice(first, first + step)
        change = corrected(inputs_ref[:, :count], panel_ref[...], aux_ref, place)
        value = product_ref[:, place] + change
        base = pl.program_id(0) * part_rows + first
        out_ref[:, place] = units_of(value, inputs_ref, where_ref, base, scale)


def tile_rows(given):
    return 2048 if given % 2048 == 0 else 1024


def eliminate(weight, factor, mask, where, product, inputs, panel_inputs, scale):
    count = 2 * BLOCK
    given = weight.shape[0]
    rows = pl.cdiv(given, 1024) * 1024
    if rows != given:
        more = ((0, rows - given), (0, 0))
        weight, mask = jnp.pad(weight[:, :count], more), jnp.pad(mask, more)
    tile = tile_rows(given)
    subs = count // SUB
    wide = factor.astype(jnp.float32)
    row = lax.broadcasted_iota(jnp.int32, wide.shape, 0)
    column = lax.broadcasted_iota(jnp.int32, wide.shape, 1)
    inverse = 1.0 / jnp.sum(jnp.where(row == column, wide, 0.0), axis=1)
    near = jnp.where(row // SUB == column // SUB, wide, 0.0)
    scalars = near.reshape(count, subs, SUB).sum(axis=1).reshape(-1)
    columns = factor.T.reshape(count, subs, SUB).transpose(1, 0, 2)
    inner = jnp.concatenate([columns, columns], 2)
    cross = factor[:BLOCK, BLOCK:].T
    cross = jnp.concatenate([cross, cross], 1)
    smem = pl.BlockSpec(memory_space=pltpu.SMEM)
    tokens = inputs.shape[0]
    part = min(given, tile)
    hbm = pltpu.MemorySpace.HBM
    pruned, aux, units = pl.pallas_call(
        functools.partial(eliminate_kernel, scale, part),
        grid=(rows // tile,),
        in_specs=[
            smem,
            smem,
            smem,
            pl.BlockSpec((subs, count, 2 * SUB), lambda i: (0, 0, 0)),
            pl.BlockSpec((BLOCK, count), lambda i: (0, 0)),
            pl.BlockSpec((tile, count), lambda i: (i, 0)),
            pl.BlockSpec((tile, count), lambda i: (i, 0)),
            pl.BlockSpec((tokens, part), lambda i: (0, i)),
            pl.BlockSpec(inputs.shape, lambda i: (0, 0)),
            pl.BlockSpec((tokens, count), lambda i: (0, 0)),
        ],
        out_specs=[
            pl.BlockSpec((tile, count), lambda i: (i, 0)),
            pl.BlockSpec((2 * count, tile), lambda i: (0, i)),
            pl.BlockSpec((tokens, part), lambda i: (0, i)),
        ],
        out_shape=[
            jax.ShapeDtypeStruct((rows, count), jnp.bfloat16),
            hbm((2 * count, rows), jnp.bfloat16),
            jax.ShapeDtypeStruct((tokens, given), jnp.bfloat16),
        ],
        scratch_shapes=[pltpu.VMEM((tile * count // 128, 128), jnp.float32)] * 3,
        compiler_params=pltpu.CompilerParams(vmem_limit_bytes=ELIMINATE_VMEM),
        cost_estimate=pl.CostEstimate(
            flops=2 * rows * count * count, bytes_accessed=rows * count * 12, transcendentals=0
        ),
        name="eliminate",
    )(
        where, scalars, inverse, inner, cross, weight,
        pltpu.with_memory_space_constraint(mask, hbm), product, inputs, panel_inputs,
    )
    return pruned[:given], aux[:, :given], units


def corrected(lead, panel_inputs, aux_ref, place):
    count = 2 * BLOCK
    tokens = lead.shape[0]
    both = nn_dot(jnp.concatenate(split_halves(panel_inputs), 0), aux_ref[count:, place])
    return nn_dot(lead, aux_ref[0:count, place]) - both[:tokens] - both[tokens:]


def units_of(value, inputs, where_ref, first, scale):
    units = (value * scale).astype(jnp.bfloat16).astype(jnp.float32)
    units = units / (1.0 + jnp.exp(-units))
    at = pl.ds(pl.multiple_of(where_ref[0] + first, 128), value.shape[1])
    units = units + inputs[:, at].astype(jnp.float32) * where_ref[1].astype(jnp.float32)
    return units.astype(jnp.bfloat16)


def fold_kernel(spread_ref, copies_ref, produced_ref):
    peers, own, features = copies_ref.shape
    rows = spread_ref.shape[2]
    parts = []
    for first in range(0, features, rows):
        part = None
        for peer in range(peers):
            if peer * rows % features == first:
                units = spread_ref[peer].astype(jnp.float32)
                part = units if part is None else part + units
        parts.append(part)
    combined = jnp.concatenate(parts, 1)
    moment = jnp.sum(combined * combined, axis=1, keepdims=True) * (1.0 / features)
    produced = (combined * lax.rsqrt(moment + epsilon)).astype(jnp.bfloat16)
    produced_ref[...] = produced
    for peer in range(peers):
        copies_ref[peer] = produced


def fold(spread, peers, features):
    own = spread.shape[1]
    return pl.pallas_call(
        fold_kernel,
        in_specs=[pl.BlockSpec(memory_space=pltpu.VMEM)],
        out_specs=[pl.BlockSpec(memory_space=pltpu.VMEM)] * 2,
        out_shape=[
            jax.ShapeDtypeStruct((peers, own, features), jnp.bfloat16),
            jax.ShapeDtypeStruct((own, features), jnp.bfloat16),
        ],
        compiler_params=pltpu.CompilerParams(vmem_limit_bytes=8 * 1024 * 1024),
        name="fold",
    )(spread)


def chunk_copy(weight_ref, target, sem, row):
    chunk, width = target.shape
    skipped = weight_ref.shape[1] - width
    return pltpu.make_async_copy(
        weight_ref.at[pl.ds(row, chunk), pl.ds(skipped, width)], target, sem
    )


def stream(weight_ref, ring, ring_sems, total, row_of, inputs, use):
    slots = ring.shape[0]

    def copy(index, slot):
        return chunk_copy(weight_ref, ring.at[slot], ring_sems.at[slot], row_of(index))

    def begin():
        for index in range(slots):
            copy(index, index).start()

    def step(index, _):
        slot = lax.rem(index, slots)
        copy(index, slot).wait()
        use(index, nt_dot(inputs(), ring[slot]))

        @pl.when(index + slots < total)
        def _():
            copy(index + slots, slot).start()

        return 0

    def run():
        lax.fori_loop(0, total, step, 0)

    return begin, run


def first_kernel(inputs_ref, weight_ref, product_ref, ring, ring_sems):
    chunk, width = ring.shape[1:]
    skipped = weight_ref.shape[1] - width

    def place_of(index):
        return pl.multiple_of(index * chunk, chunk)

    def use(index, product):
        product_ref[:, pl.ds(place_of(index), chunk)] = product

    total = product_ref.shape[1] // chunk
    begin, run = stream(
        weight_ref, ring, ring_sems, total, place_of, lambda: inputs_ref[:, skipped:], use
    )
    begin()
    run()


def first_product(inputs, weight):
    tokens, features = inputs.shape
    rows = weight.shape[0]
    width = features - 2 * BLOCK
    chunk = min(256, rows // 2)
    ring = (min(6, rows // chunk), chunk, width)
    return pl.pallas_call(
        first_kernel,
        in_specs=[
            pl.BlockSpec(memory_space=pltpu.VMEM),
            pl.BlockSpec(memory_space=pltpu.MemorySpace.HBM),
        ],
        out_specs=pl.BlockSpec(memory_space=pltpu.VMEM),
        out_shape=jax.ShapeDtypeStruct((tokens, rows), jnp.float32),
        scratch_shapes=[pltpu.VMEM(ring, jnp.bfloat16), pltpu.SemaphoreType.DMA((ring[0],))],
        compiler_params=pltpu.CompilerParams(vmem_limit_bytes=32 * 1024 * 1024),
        cost_estimate=pl.CostEstimate(
            flops=2 * tokens * rows * width, bytes_accessed=rows * width * 2, transcendentals=0
        ),
        name="first_product",
    )(inputs, weight)


def turn_kernel(scale, where_ref, inputs_ref, weight_ref, panel_ref, aux_ref, out_ref, ring, panel,
                aux, change, ring_sems, side_sems):
    chunk, width = ring.shape[1:]
    skipped = weight_ref.shape[1] - width

    def place_of(index):
        return pl.multiple_of(index * chunk, chunk)

    def use(index, product):
        place = pl.ds(place_of(index), chunk)
        value = product + change[:, place]
        out_ref[:, place] = units_of(value, inputs_ref, where_ref, place_of(index), scale)

    rows = change.shape[1]
    begin, run = stream(
        weight_ref, ring, ring_sems, rows // chunk, place_of, lambda: inputs_ref[:, skipped:], use
    )
    panel_copy = pltpu.make_async_copy(
        panel_ref.at[:, pl.ds(skipped, width)], panel, side_sems.at[0]
    )
    aux_copy = pltpu.make_async_copy(aux_ref, aux, side_sems.at[1])
    panel_copy.start()
    aux_copy.start()
    begin()
    panel_copy.wait()
    panel_inputs = nt_dot(inputs_ref[:, skipped:], panel[...])
    aux_copy.wait()
    step = min(1024, rows)
    for first in range(0, rows, step):
        place = slice(first, first + step)
        change[:, place] = corrected(inputs_ref[:, :skipped], panel_inputs, aux, place)
    run()


def turn_product(where, inputs, weight, panel, aux, scale):
    tokens, features = inputs.shape
    rows = weight.shape[0]
    count = 2 * BLOCK
    width = features - count
    chunk = min(256, rows // 2)
    ring = (min(6, rows // chunk), chunk, width)
    vmem = pl.BlockSpec(memory_space=pltpu.VMEM)
    hbm = pl.BlockSpec(memory_space=pltpu.MemorySpace.HBM)
    return pl.pallas_call(
        functools.partial(turn_kernel, scale),
        in_specs=[pl.BlockSpec(memory_space=pltpu.SMEM), vmem, hbm, hbm, hbm],
        out_specs=vmem,
        out_shape=jax.ShapeDtypeStruct((tokens, rows), jnp.bfloat16),
        scratch_shapes=[
            pltpu.VMEM(ring, jnp.bfloat16),
            pltpu.VMEM((count, width), jnp.bfloat16),
            pltpu.VMEM(aux.shape, jnp.bfloat16),
            pltpu.VMEM((tokens, rows), jnp.float32),
            pltpu.SemaphoreType.DMA((ring[0],)),
            pltpu.SemaphoreType.DMA((2,)),
        ],
        compiler_params=pltpu.CompilerParams(vmem_limit_bytes=TURN_VMEM),
        cost_estimate=pl.CostEstimate(
            flops=2 * tokens * rows * features, bytes_accessed=rows * width * 2, transcendentals=0
        ),
        name="turn_product",
    )(
        where, inputs, weight,
        *(pltpu.with_memory_space_constraint(a, pltpu.MemorySpace.HBM) for a in (panel, aux)),
    )


def per_device(tokens, up_weight, hess_panel, keep_mask):
    weight = up_weight[0]
    local_panel = hess_panel[0].astype(jnp.bfloat16)
    count = 2 * BLOCK
    features = weight.shape[1]
    scale = features ** (-0.5)
    row_size = lax.axis_size("row")
    own = tokens.shape[0]
    held = local_panel.shape[1]
    position = lax.axis_index("layer")
    depth = lax.axis_size("layer")
    start = lax.axis_index("row") * held

    width = min(count, held)
    share = count // row_size
    factor_share = local_panel[:, :width].reshape(row_size, share * width // count, count)
    cut = own * features // count
    token_share = jnp.broadcast_to(tokens.reshape(1, cut, count), (row_size, cut, count))
    first = lax.all_to_all(
        jnp.concatenate([token_share, factor_share], 1), "row", split_axis=0, concat_axis=0
    )
    first, local_panel = lax.optimization_barrier((first, local_panel))
    portion = first[:, :cut].reshape(row_size * own, features)
    full_panel = lax.all_gather(local_panel, "row", axis=1, tiled=True)

    owned = [first[o, cut:].reshape(share, width) for o in range(count // width)]
    column = lax.broadcasted_iota(jnp.int32, local_panel.shape, 1) + start
    remote = jnp.where(column < count, jnp.zeros_like(local_panel), local_panel)
    partial_sum = nt_dot(lax.dynamic_slice_in_dim(portion, start, held, 1), remote)
    shares = jnp.concatenate([jnp.concatenate(owned, 1), *split_halves(partial_sum)], 0)
    shares, portion = lax.optimization_barrier((shares, portion))
    second = gathered(shares, "row")
    factor = second[:, :share].reshape(count, count)
    sums = second[:, share:].astype(jnp.float32).reshape(row_size, 2, row_size * own, count)

    product = first_product(portion, weight)
    rows = weight.shape[0]
    from_row = lax.axis_index("row") * rows
    where = jnp.stack([from_row % features, (from_row < features).astype(jnp.int32)])
    pruned, aux, units = eliminate(
        weight, factor, keep_mask[0], where, product, portion, sums.sum(axis=(0, 1)), scale
    )
    results = jnp.zeros_like(tokens)
    for turn in range(depth):
        last = turn + 1 == depth
        if turn:
            portion = copies.reshape(row_size * own, features)
            units = turn_product(where, portion, weight, full_panel, aux, scale)
        units = units.reshape(row_size, own, rows)
        if last:
            spread = lax.all_to_all(units, "row", split_axis=0, concat_axis=0)
        else:
            pair = [turn, turn + 1]
            others = [layer for layer in range(depth) if layer not in pair]
            groups = [
                [layer * row_size + peer for layer in layers for peer in range(row_size)]
                for layers in [pair] + [others[i : i + 2] for i in range(0, len(others), 2)]
            ]
            spread = lax.all_to_all(
                jnp.concatenate([units, units], 0), ("layer", "row"), split_axis=0, concat_axis=0, axis_index_groups=groups
            )
        copies, produced = fold(spread, row_size, features)
        results = jnp.where(position == turn, produced, results)
        if not last:
            copies = lax.all_to_all(copies, "row", split_axis=0, concat_axis=0)
    return (results[None], pruned[None])


def solution(mesh):
    in_specs = (
        P("row", None),
        P("layer", "row", None),
        P("layer", None, "row"),
        P("layer", "row", None),
    )
    out_specs = (P("layer", "row", None), P("layer", "row", None))
    return jax.shard_map(
        per_device, mesh=mesh, in_specs=in_specs, out_specs=out_specs, check_vma=False
    )
```

```python
import functools

import jax
import jax.numpy as jnp
from jax import lax
from jax.experimental import pallas as pl
from jax.experimental.pallas import tpu as pltpu
from jax.sharding import PartitionSpec as P

BLOCK = 128
SUB = 16
ELIMINATE_VMEM = 40 * 1024 * 1024
TURN_VMEM = 36 * 1024 * 1024

epsilon = 1e-05


def gathered(array, axis):
    size = lax.axis_size(axis)
    copies = jnp.broadcast_to(array[None], (size,) + array.shape)
    return lax.all_to_all(copies, axis, split_axis=0, concat_axis=0)


def nt_dot(left, right):
    return lax.dot_general(
        left, right, (((1,), (1,)), ((), ())), preferred_element_type=jnp.float32
    )


def nn_dot(left, right):
    return jnp.dot(left, right, preferred_element_type=jnp.float32)


def split_halves(value):
    high = value.astype(jnp.bfloat16)
    low = (value - high.astype(jnp.float32)).astype(jnp.bfloat16)
    return high, low


def identity(count):
    row = lax.broadcasted_iota(jnp.int32, (count, count), 0)
    column = lax.broadcasted_iota(jnp.int32, (count, count), 1)
    return jnp.where(row == column, 1.0, 0.0).astype(jnp.bfloat16)


def eliminate_kernel(scale, part_rows, where_ref, scalar_ref, inverse_ref, inner_ref, cross_ref, weight_ref,
                     mask_ref, product_ref, inputs_ref, panel_ref, pruned_ref, aux_ref, out_ref,
                     state, dropped, errors):
    count = 2 * BLOCK
    depth = count * 8
    sheets = state.shape[0] // depth
    lanes = sheets * 128
    spots = [(g, q, slice((g * sheets + q) * 128, (g * sheets + q + 1) * 128))
             for g in range(8) for q in range(sheets)]

    def place(g, q, first, size):
        return pl.ds(q * depth + first * 8 + g, size, stride=8)

    def plane(q, j):
        return slice(q * depth + j * 8, q * depth + (j + 1) * 8)

    eye = identity(count)
    columns = nt_dot(eye, weight_ref[...])
    drops = nt_dot(eye, (1 - mask_ref[...]).astype(jnp.float32).astype(jnp.bfloat16))
    for g, q, where in spots:
        state[place(g, q, 0, count), :] = columns[:, where]
        dropped[place(g, q, 0, count), :] = drops[:, where]

    def stacked(first, size):
        wide = jnp.concatenate([errors[place(g, q, first, size), :] for g, q, _ in spots], 1)
        return jnp.concatenate(split_halves(wide), 0)

    def subtract(product, first, size):
        for g, q, where in spots:
            at = place(g, q, first, size)
            state[at, :] = state[at, :] - product[:, where]

    for block in range(2):
        for part in range(BLOCK // SUB):
            first = block * BLOCK + part * SUB
            planes = [[state[plane(q, first + i), :] for q in range(sheets)] for i in range(SUB)]
            for i in range(SUB):
                j = first + i
                inverse = inverse_ref[j]
                error = []
                for q in range(sheets):
                    lost = planes[i][q] * dropped[plane(q, j), :]
                    error.append(lost * inverse)
                    state[plane(q, j), :] = planes[i][q] - lost
                    errors[plane(q, j), :] = error[q]
                for k in range(i + 1, SUB):
                    scalar = scalar_ref[j * SUB + k]
                    for q in range(sheets):
                        planes[k][q] = planes[k][q] - error[q] * scalar
            after = first + SUB
            left = (block + 1) * BLOCK - after
            if left:
                factor = inner_ref[block * (BLOCK // SUB) + part, after : after + left, :]
                subtract(nn_dot(factor, stacked(first, SUB)), after, left)
        if block == 0:
            subtract(nn_dot(cross_ref[...], stacked(0, BLOCK)), BLOCK, BLOCK)

    small = identity(128)
    for g, q, where in spots:
        kept = state[place(g, q, 0, count), :].astype(jnp.bfloat16)
        aux_ref[0:count, where] = kept
        aux_ref[count:, where] = errors[place(g, q, 0, count), :].astype(jnp.bfloat16)
        pruned_ref[where, :] = nt_dot(small, kept).astype(jnp.bfloat16)

    step = min(512, part_rows)
    for first in range(0, part_rows, step):
        place = slice(first, first + step)
        change = corrected(inputs_ref[:, :count], panel_ref[...], aux_ref, place)
        value = product_ref[:, place] + change
        base = pl.program_id(0) * part_rows + first
        out_ref[:, place] = units_of(value, inputs_ref, where_ref, base, scale)


def tile_rows(given):
    return 2048 if given % 2048 == 0 else 1024


def eliminate(weight, factor, mask, where, product, inputs, panel_inputs, scale):
    count = 2 * BLOCK
    given = weight.shape[0]
    rows = pl.cdiv(given, 1024) * 1024
    if rows != given:
        more = ((0, rows - given), (0, 0))
        weight, mask = jnp.pad(weight[:, :count], more), jnp.pad(mask, more)
    tile = tile_rows(given)
    subs = count // SUB
    wide = factor.astype(jnp.float32)
    row = lax.broadcasted_iota(jnp.int32, wide.shape, 0)
    column = lax.broadcasted_iota(jnp.int32, wide.shape, 1)
    inverse = 1.0 / jnp.sum(jnp.where(row == column, wide, 0.0), axis=1)
    near = jnp.where(row // SUB == column // SUB, wide, 0.0)
    scalars = near.reshape(count, subs, SUB).sum(axis=1).reshape(-1)
    columns = factor.T.reshape(count, subs, SUB).transpose(1, 0, 2)
    inner = jnp.concatenate([columns, columns], 2)
    cross = factor[:BLOCK, BLOCK:].T
    cross = jnp.concatenate([cross, cross], 1)
    smem = pl.BlockSpec(memory_space=pltpu.SMEM)
    tokens = inputs.shape[0]
    part = min(given, tile)
    hbm = pltpu.MemorySpace.HBM
    pruned, aux, units = pl.pallas_call(
        functools.partial(eliminate_kernel, scale, part),
        grid=(rows // tile,),
        in_specs=[
            smem,
            smem,
            smem,
            pl.BlockSpec((subs, count, 2 * SUB), lambda i: (0, 0, 0)),
            pl.BlockSpec((BLOCK, count), lambda i: (0, 0)),
            pl.BlockSpec((tile, count), lambda i: (i, 0)),
            pl.BlockSpec((tile, count), lambda i: (i, 0)),
            pl.BlockSpec((tokens, part), lambda i: (0, i)),
            pl.BlockSpec(inputs.shape, lambda i: (0, 0)),
            pl.BlockSpec((tokens, count), lambda i: (0, 0)),
        ],
        out_specs=[
            pl.BlockSpec((tile, count), lambda i: (i, 0)),
            pl.BlockSpec((2 * count, tile), lambda i: (0, i)),
            pl.BlockSpec((tokens, part), lambda i: (0, i)),
        ],
        out_shape=[
            jax.ShapeDtypeStruct((rows, count), jnp.bfloat16),
            hbm((2 * count, rows), jnp.bfloat16),
            jax.ShapeDtypeStruct((tokens, given), jnp.bfloat16),
        ],
        scratch_shapes=[pltpu.VMEM((tile * count // 128, 128), jnp.float32)] * 3,
        compiler_params=pltpu.CompilerParams(vmem_limit_bytes=ELIMINATE_VMEM),
        cost_estimate=pl.CostEstimate(
            flops=2 * rows * count * count, bytes_accessed=rows * count * 12, transcendentals=0
        ),
        name="eliminate",
    )(
        where, scalars, inverse, inner, cross, weight,
        pltpu.with_memory_space_constraint(mask, hbm), product, inputs, panel_inputs,
    )
    return pruned[:given], aux[:, :given], units


def corrected(lead, panel_inputs, aux_ref, place):
    count = 2 * BLOCK
    tokens = lead.shape[0]
    both = nn_dot(jnp.concatenate(split_halves(panel_inputs), 0), aux_ref[count:, place])
    return nn_dot(lead, aux_ref[0:count, place]) - both[:tokens] - both[tokens:]


def units_of(value, inputs, where_ref, first, scale):
    units = (value * scale).astype(jnp.bfloat16).astype(jnp.float32)
    units = units / (1.0 + jnp.exp(-units))
    at = pl.ds(pl.multiple_of(where_ref[0] + first, 128), value.shape[1])
    units = units + inputs[:, at].astype(jnp.float32) * where_ref[1].astype(jnp.float32)
    return units.astype(jnp.bfloat16)


def fold_kernel(spread_ref, copies_ref, produced_ref):
    peers, own, features = copies_ref.shape
    rows = spread_ref.shape[2]
    parts = []
    for first in range(0, features, rows):
        part = None
        for peer in range(peers):
            if peer * rows % features == first:
                units = spread_ref[peer].astype(jnp.float32)
                part = units if part is None else part + units
        parts.append(part)
    combined = jnp.concatenate(parts, 1)
    moment = jnp.sum(combined * combined, axis=1, keepdims=True) * (1.0 / features)
    produced = (combined * lax.rsqrt(moment + epsilon)).astype(jnp.bfloat16)
    produced_ref[...] = produced
    for peer in range(peers):
        copies_ref[peer] = produced


def fold(spread, peers, features):
    own = spread.shape[1]
    return pl.pallas_call(
        fold_kernel,
        in_specs=[pl.BlockSpec(memory_space=pltpu.VMEM)],
        out_specs=[pl.BlockSpec(memory_space=pltpu.VMEM)] * 2,
        out_shape=[
            jax.ShapeDtypeStruct((peers, own, features), jnp.bfloat16),
            jax.ShapeDtypeStruct((own, features), jnp.bfloat16),
        ],
        compiler_params=pltpu.CompilerParams(vmem_limit_bytes=8 * 1024 * 1024),
        name="fold",
    )(spread)


def chunk_copy(weight_ref, target, sem, row):
    chunk, width = target.shape
    skipped = weight_ref.shape[1] - width
    return pltpu.make_async_copy(
        weight_ref.at[pl.ds(row, chunk), pl.ds(skipped, width)], target, sem
    )


def stream(weight_ref, ring, ring_sems, total, row_of, inputs):
    slots = ring.shape[0]

    def copy(index, slot):
        return chunk_copy(weight_ref, ring.at[slot], ring_sems.at[slot], row_of(index))

    ahead = slots - 1

    def begin():
        for index in range(ahead):
            copy(index, index).start()

    def run(first, last, use, besides=None):
        def step(index, _):
            slot = lax.rem(index, slots)
            copy(index, slot).wait()

            @pl.when(index + ahead < total)
            def _():
                copy(index + ahead, lax.rem(index + ahead, slots)).start()

            if besides is not None:
                pl.when(index == first)(besides)
            use(index, nt_dot(inputs(), ring[slot]))
            return 0

        lax.fori_loop(first, last, step, 0)

    return begin, run


def first_kernel(inputs_ref, weight_ref, product_ref, ring, ring_sems):
    chunk, width = ring.shape[1:]
    skipped = weight_ref.shape[1] - width

    def place_of(index):
        return pl.multiple_of(index * chunk, chunk)

    def use(index, product):
        product_ref[:, pl.ds(place_of(index), chunk)] = product

    total = product_ref.shape[1] // chunk
    begin, run = stream(
        weight_ref, ring, ring_sems, total, place_of, lambda: inputs_ref[:, skipped:]
    )
    begin()
    run(0, total, use)


def first_product(inputs, weight):
    tokens, features = inputs.shape
    rows = weight.shape[0]
    width = features - 2 * BLOCK
    chunk = min(256, rows // 2)
    ring = (min(4, rows // chunk), chunk, width)
    return pl.pallas_call(
        first_kernel,
        in_specs=[
            pl.BlockSpec(memory_space=pltpu.VMEM),
            pl.BlockSpec(memory_space=pltpu.MemorySpace.HBM),
        ],
        out_specs=pl.BlockSpec(memory_space=pltpu.VMEM),
        out_shape=jax.ShapeDtypeStruct((tokens, rows), jnp.float32),
        scratch_shapes=[pltpu.VMEM(ring, jnp.bfloat16), pltpu.SemaphoreType.DMA((ring[0],))],
        compiler_params=pltpu.CompilerParams(vmem_limit_bytes=32 * 1024 * 1024),
        cost_estimate=pl.CostEstimate(
            flops=2 * tokens * rows * width, bytes_accessed=rows * width * 2, transcendentals=0
        ),
        name="first_product",
    )(inputs, weight)


def turn_kernel(scale, where_ref, inputs_ref, weight_ref, panel_ref, aux_ref, out_ref, ring, panel,
                aux, change, ring_sems, side_sems):
    chunk, width = ring.shape[1:]
    skipped = weight_ref.shape[1] - width

    def place_of(index):
        return pl.multiple_of(index * chunk, chunk)

    def use(index, product):
        place = pl.ds(place_of(index), chunk)
        value = product + change[:, place]
        out_ref[:, place] = units_of(value, inputs_ref, where_ref, place_of(index), scale)

    def keep(index, product):
        change[:, pl.ds(place_of(index), chunk)] = product

    rows = change.shape[1]
    total = rows // chunk
    early = total // 2
    begin, run = stream(
        weight_ref, ring, ring_sems, total, place_of, lambda: inputs_ref[:, skipped:]
    )
    panel_copy = pltpu.make_async_copy(
        panel_ref.at[:, pl.ds(skipped, width)], panel, side_sems.at[0]
    )
    aux_copy = pltpu.make_async_copy(aux_ref, aux, side_sems.at[1])

    def start_sides():
        panel_copy.start()
        aux_copy.start()

    begin()
    run(0, early, keep, start_sides)
    panel_copy.wait()
    panel_inputs = nt_dot(inputs_ref[:, skipped:], panel[...])
    aux_copy.wait()
    step = min(1024, early * chunk)
    for first in range(0, rows, step):
        place = slice(first, first + step)
        part = corrected(inputs_ref[:, :skipped], panel_inputs, aux, place)
        if first < early * chunk:
            value = change[:, place] + part
            out_ref[:, place] = units_of(value, inputs_ref, where_ref, first, scale)
        else:
            change[:, place] = part
    run(early, total, use)


def turn_product(where, inputs, weight, panel, aux, scale):
    tokens, features = inputs.shape
    rows = weight.shape[0]
    count = 2 * BLOCK
    width = features - count
    chunk = min(256, rows // 2)
    ring = (min(4, rows // chunk), chunk, width)
    vmem = pl.BlockSpec(memory_space=pltpu.VMEM)
    hbm = pl.BlockSpec(memory_space=pltpu.MemorySpace.HBM)
    return pl.pallas_call(
        functools.partial(turn_kernel, scale),
        in_specs=[pl.BlockSpec(memory_space=pltpu.SMEM), vmem, hbm, hbm, hbm],
        out_specs=vmem,
        out_shape=jax.ShapeDtypeStruct((tokens, rows), jnp.bfloat16),
        scratch_shapes=[
            pltpu.VMEM(ring, jnp.bfloat16),
            pltpu.VMEM((count, width), jnp.bfloat16),
            pltpu.VMEM(aux.shape, jnp.bfloat16),
            pltpu.VMEM((tokens, rows), jnp.float32),
            pltpu.SemaphoreType.DMA((ring[0],)),
            pltpu.SemaphoreType.DMA((2,)),
        ],
        compiler_params=pltpu.CompilerParams(vmem_limit_bytes=TURN_VMEM),
        cost_estimate=pl.CostEstimate(
            flops=2 * tokens * rows * features, bytes_accessed=rows * width * 2, transcendentals=0
        ),
        name="turn_product",
    )(
        where, inputs, weight,
        *(pltpu.with_memory_space_constraint(a, pltpu.MemorySpace.HBM) for a in (panel, aux)),
    )


def per_device(tokens, up_weight, hess_panel, keep_mask):
    weight = up_weight[0]
    local_panel = hess_panel[0].astype(jnp.bfloat16)
    count = 2 * BLOCK
    features = weight.shape[1]
    scale = features ** (-0.5)
    row_size = lax.axis_size("row")
    own = tokens.shape[0]
    held = local_panel.shape[1]
    position = lax.axis_index("layer")
    depth = lax.axis_size("layer")
    start = lax.axis_index("row") * held

    width = min(count, held)
    share = count // row_size
    factor_share = local_panel[:, :width].reshape(row_size, share * width // count, count)
    cut = own * features // count
    token_share = jnp.broadcast_to(tokens.reshape(1, cut, count), (row_size, cut, count))
    first = lax.all_to_all(
        jnp.concatenate([token_share, factor_share], 1), "row", split_axis=0, concat_axis=0
    )
    first, local_panel = lax.optimization_barrier((first, local_panel))
    portion = first[:, :cut].reshape(row_size * own, features)
    full_panel = lax.all_gather(local_panel, "row", axis=1, tiled=True)

    owned = [first[o, cut:].reshape(share, width) for o in range(count // width)]
    column = lax.broadcasted_iota(jnp.int32, local_panel.shape, 1) + start
    remote = jnp.where(column < count, jnp.zeros_like(local_panel), local_panel)
    partial_sum = nt_dot(lax.dynamic_slice_in_dim(portion, start, held, 1), remote)
    shares = jnp.concatenate([jnp.concatenate(owned, 1), *split_halves(partial_sum)], 0)
    shares, portion = lax.optimization_barrier((shares, portion))
    second = gathered(shares, "row")
    factor = second[:, :share].reshape(count, count)
    sums = second[:, share:].astype(jnp.float32).reshape(row_size, 2, row_size * own, count)

    product = first_product(portion, weight)
    rows = weight.shape[0]
    from_row = lax.axis_index("row") * rows
    where = jnp.stack([from_row % features, (from_row < features).astype(jnp.int32)])
    pruned, aux, units = eliminate(
        weight, factor, keep_mask[0], where, product, portion, sums.sum(axis=(0, 1)), scale
    )
    results = jnp.zeros_like(tokens)
    for turn in range(depth):
        last = turn + 1 == depth
        if turn:
            portion = copies.reshape(row_size * own, features)
            units = turn_product(where, portion, weight, full_panel, aux, scale)
        units = units.reshape(row_size, own, rows)
        if last:
            spread = lax.all_to_all(units, "row", split_axis=0, concat_axis=0)
        else:
            pair = [turn, turn + 1]
            others = [layer for layer in range(depth) if layer not in pair]
            groups = [
                [layer * row_size + peer for layer in layers for peer in range(row_size)]
                for layers in [pair] + [others[i : i + 2] for i in range(0, len(others), 2)]
            ]
            spread = lax.all_to_all(
                jnp.concatenate([units, units], 0), ("layer", "row"), split_axis=0, concat_axis=0, axis_index_groups=groups
            )
        copies, produced = fold(spread, row_size, features)
        results = jnp.where(position == turn, produced, results)
        if not last:
            copies = lax.all_to_all(copies, "row", split_axis=0, concat_axis=0)
    return (results[None], pruned[None])


def solution(mesh):
    in_specs = (
        P("row", None),
        P("layer", "row", None),
        P("layer", None, "row"),
        P("layer", "row", None),
    )
    out_specs = (P("layer", "row", None), P("layer", "row", None))
    return jax.shard_map(
        per_device, mesh=mesh, in_specs=in_specs, out_specs=out_specs, check_vma=False
    )
```
